128 devices in a mesh: row: 8 (over y, z_hi), col: 16 (over x, z_lo, core).
Axes of the slice: x: 4, y: 4, z: 4 (z_hi: 2, z_lo: 2; z = z_hi * 2 + z_lo), core: 2. Of those that a mesh axis runs over, the one named last changes fastest.
Arguments:
- owned_blocks: bfloat16 [2048, 16, 128, 128], P(('row', 'col')), may hold values from -0.8984375 to 0.8984375
- owned_rows: int32 [2048], P(('row', 'col')), may hold values from 0 to 64, as said below
- owned_cols: int32 [2048, 16], P(('row', 'col')), may hold values from 0 to 31
- keep: int32 [16, 512], P('row', 'col'), may hold values 0 or 1
Outputs:
- purified: bfloat16 [2048, 65536], P('row', 'col')
The draws below stay inside these ranges and needn't reach their ends.
Inputs may be any that keep to these rules, and one draw needn't show every extreme that they name: `owned_rows`: every block row of P stands in exactly one slot, in a slot of its own band; in every band some owner fills all 2 of its slots for that band.
All inputs are finite; a program needn't handle non-finite values. No bound on the sum of `keep` on one device may be relied on, other than what follows from the above.
Results may differ from the reference program's by a relative error of at most 0.005.
Values may be sent and summed in bfloat16 or wider, within the bound.
No kernel may reach another device: no remote copies, remote signals or barrier semaphores. Data moves between devices by JAX's collectives and lax.ppermute only.
A program may use at most 256 MiB of HBM per device.

```python
import jax
import jax.numpy as jnp
from jax import lax

BLK = 128
GCOL = 32
RLOC = 2
NB = 512
HB = 64
W = 16
BANDCAP = 2
OWNSLOTS = 16
N_ROW = 8
N_COL = 16
DEVICES = 128


def draw_owned_rows(key, part):
    band_rows = 2 * GCOL
    full_count = band_rows // (2 * BANDCAP)
    remaining = band_rows - full_count * BANDCAP
    others = DEVICES - full_count
    base_share = remaining // others
    extra_share = remaining % others
    position = jnp.arange(DEVICES, dtype=jnp.int32)
    later = position - full_count
    counts = jnp.where(position < full_count, BANDCAP, base_share + (later < extra_share).astype(jnp.int32))
    starts = jnp.cumsum(counts) - counts
    slot_ids = jnp.arange(BANDCAP, dtype=jnp.int32)

    def one_band(band_id):
        band_key = jax.random.fold_in(key, 17 + band_id)
        owner_order = jax.random.permutation(jax.random.fold_in(band_key, 1), DEVICES)
        row_order = jax.random.permutation(jax.random.fold_in(band_key, 2), band_rows).astype(jnp.int32)
        spots = starts[:, None] + slot_ids[None, :]
        values = jnp.where(slot_ids[None, :] < counts[:, None], row_order[jnp.minimum(spots, band_rows - 1)], band_rows)
        return jnp.zeros((DEVICES, BANDCAP), jnp.int32).at[owner_order].set(values.astype(jnp.int32))
    tables = jax.vmap(one_band)(jnp.arange(N_ROW, dtype=jnp.int32))
    return tables.transpose(1, 0, 2).reshape(DEVICES * N_ROW * BANDCAP).astype(jnp.int32)


def with_ends(entries, key, least, top_value):
    place = [jax.random.randint(jax.random.fold_in(key, axis), (), 0, length) for axis, length in enumerate(entries.shape)]
    main_axis = entries.shape.index(max(entries.shape))
    next_to = place[:main_axis] + [(place[main_axis] + 1) % entries.shape[main_axis]] + place[main_axis + 1:]
    return entries.at[tuple(place)].set(least).at[tuple(next_to)].set(top_value)


def block_levels(stream_key, dims, split, least, largest):
    factor_of, own = 1.0, jax.random.fold_in(stream_key, 6)
    for dim, shards_of in split:
        draws = jnp.exp(jax.random.uniform(jax.random.fold_in(own, dim), (shards_of,), jnp.float32, least / len(split), largest / len(split)))
        factor_of = factor_of * jnp.repeat(draws, dims[dim] // shards_of).reshape([-1 if axis == dim else 1 for axis in range(len(dims))])
    return factor_of


def bell_draw(stream_key, dims, deviation, most, cuts=(), kind=jnp.bfloat16):
    array = jax.random.normal(stream_key, dims, jnp.float32) * deviation
    if len(cuts) > 0:
        array = block_levels(stream_key, dims, cuts, -0.22, 0.18) * array
    return jnp.clip(array, min=-most, max=most).astype(kind)


def setup_inputs(seed: int = 0) -> dict:
    seeds = jax.random.split(jax.random.key(seed), 5)
    owned_blocks = bell_draw(seeds[0], (DEVICES * OWNSLOTS, N_COL, BLK, BLK), 0.15, 0.8984375, ((0, 128),))
    owned_rows = draw_owned_rows(jax.random.fold_in(seeds[4], 71), 0)
    owned_cols = with_ends(jax.random.randint(seeds[2], (DEVICES * OWNSLOTS, N_COL), 0, GCOL), jax.random.fold_in(seeds[2], 1), 0, GCOL - 1).astype(jnp.int32)
    keep = with_ends((jax.random.randint(seeds[3], (W, NB), 0, 8) < 7).astype(jnp.int32), jax.random.fold_in(seeds[3], 1), 0, 1)
    return dict(owned_blocks=owned_blocks, owned_rows=owned_rows, owned_cols=owned_cols, keep=keep)


def build_matrix(owned_blocks, owned_rows, owned_cols):
    slot_count = owned_rows.shape[0]
    band_ids = (jnp.arange(slot_count).astype(jnp.int32) // BANDCAP) % N_ROW
    row_ids = GCOL * (band_ids + N_ROW * (owned_rows // GCOL)) + owned_rows % GCOL
    row_ids = jnp.where(owned_rows < HB, row_ids, NB).astype(jnp.int32)
    blocks = jnp.zeros((NB, N_COL, BLK, BLK), jnp.bfloat16).at[row_ids].set(owned_blocks, mode="drop")
    columns = jnp.zeros((NB, N_COL), jnp.int32).at[row_ids].set(owned_cols, mode="drop")
    return blocks, columns


def reference(owned_blocks, owned_rows, owned_cols, keep):
    blocks, columns = build_matrix(owned_blocks, owned_rows, owned_cols)
    group_base = (GCOL * jnp.arange(N_COL)).astype(jnp.int32)
    window_ids = jnp.arange(W).astype(jnp.int32)
    window = (GCOL * (window_ids // RLOC) + window_ids % RLOC).astype(jnp.int32)
    left_blocks = blocks[window].astype(jnp.float32)
    inner_rows = (group_base[None, :] + columns[window]).astype(jnp.int32)
    right_blocks = blocks[inner_rows].astype(jnp.float32)
    targets = (group_base[None, None, :] + columns[inner_rows]).astype(jnp.int32)
    products = jnp.einsum("wgab,wghbc->wghac", left_blocks, right_blocks, precision=lax.Precision.HIGHEST)
    row_index = jnp.broadcast_to(window_ids[:, None, None], targets.shape)
    square = jnp.zeros((W, NB, BLK, BLK), jnp.float32).at[row_index, targets].add(products)
    keep_mask = keep.astype(jnp.float32)[:, :, None, None]
    filtered = (square * keep_mask).astype(jnp.bfloat16)

    def add_row(running, inner_id):
        left_piece = lax.dynamic_index_in_dim(filtered, inner_id, 1, keepdims=False).astype(jnp.float32)
        right_piece = blocks[inner_id].astype(jnp.float32)
        partial_terms = jnp.einsum("wab,gbc->wgac", left_piece, right_piece, precision=lax.Precision.HIGHEST)
        spots = (group_base + columns[inner_id]).astype(jnp.int32)
        return running.at[:, spots].add(partial_terms), None

    cubed, _ = lax.scan(add_row, jnp.zeros((W, NB, BLK, BLK), jnp.float32), jnp.arange(NB).astype(jnp.int32))
    purified = (3.0 * filtered.astype(jnp.float32) - 2.0 * cubed).astype(jnp.bfloat16)
    return purified.transpose(0, 2, 1, 3).reshape(W * BLK, NB * BLK)
```

```python
import functools

import jax
import jax.numpy as jnp
from jax import lax
from jax.experimental import pallas as pl
from jax.experimental.pallas import tpu as pltpu
from jax.sharding import PartitionSpec as P

AXES = ("row", "col")
B = 128
ROWS, COLS = 8, 16
GROUP = 32
MIB = 1 << 20


def moved(by_y, flip_z):
    pairs = []
    for r in range(ROWS):
        y, z = r // 2, r % 2
        pairs.append((r, (y + by_y) % 4 * 2 + (z ^ flip_z)))
    return pairs


def send_row(value, by_y, flip_z):
    return lax.ppermute(value, "row", moved(by_y, flip_z))


def pack_kernel(where, arrived, band, inner, window, sems):
    def one(source, target, sem):
        pltpu.make_async_copy(arrived.at[source], target, sem).start()

    @pl.loop(0, 2)
    def _(n):
        one(where[n], window.at[n], sems.at[2])

    @pl.loop(0, 32)
    def _(n):
        one(where[64 + n], inner.at[n], sems.at[1])

    @pl.loop(0, 64)
    def _(n):
        one(where[n], band.at[n], sems.at[0])

    for n, target in enumerate((band, inner, window)):
        pltpu.make_async_copy(
            arrived.at[pl.ds(0, target.shape[0])], target, sems.at[n]
        ).wait()


def pack(where, arrived):
    shapes = [jax.ShapeDtypeStruct((n, B, B), jnp.bfloat16) for n in (64, 32, 2)]
    return pl.pallas_call(
        pack_kernel,
        grid_spec=pltpu.PrefetchScalarGridSpec(
            num_scalar_prefetch=1,
            grid=(),
            in_specs=[pl.BlockSpec(memory_space=pl.ANY)],
            out_specs=[pl.BlockSpec(memory_space=pltpu.VMEM)] * 3,
            scratch_shapes=[pltpu.SemaphoreType.DMA((3,))],
        ),
        out_shape=shapes,
        compiler_params=pltpu.CompilerParams(vmem_limit_bytes=16 * MIB),
        cost_estimate=pl.CostEstimate(flops=0, bytes_accessed=6 * MIB, transcendentals=0),
        name="pack",
    )(where, arrived)


def square_kernel(leader, mask, left, inner, *refs):
    out, total = refs[-2:]
    total[...] = jnp.zeros_like(total)
    for g in range(COLS):
        for i in range(2):
            at = leader[i * 16 + g]
            total[i * 16 + at] += jnp.dot(
                left[g, i],
                inner[g % ROWS, i, g // ROWS],
                preferred_element_type=jnp.float32,
            )
    for n in range(32):
        out[n] = (total[n] * mask[n].astype(jnp.float32)).astype(jnp.bfloat16)


def square(leader, mask, left, inner, first):
    return pl.pallas_call(
        square_kernel,
        grid_spec=pltpu.PrefetchScalarGridSpec(
            num_scalar_prefetch=2,
            grid=(),
            in_specs=[pl.BlockSpec(memory_space=pltpu.VMEM)] * 2
            + [pl.BlockSpec(memory_space=pl.ANY)] * len(first),
            out_specs=pl.BlockSpec(memory_space=pltpu.VMEM),
            scratch_shapes=[pltpu.VMEM((32, B, B), jnp.float32)],
        ),
        out_shape=jax.ShapeDtypeStruct((32, B, B), jnp.bfloat16),
        compiler_params=pltpu.CompilerParams(vmem_limit_bytes=16 * MIB),
        cost_estimate=pl.CostEstimate(
            flops=32 * 2 * B**3, bytes_accessed=3 * MIB, transcendentals=0
        ),
        name="square",
    )(leader, mask, left, inner, *first)


def cubed_kernel(groups, inner_at, target, *refs):
    filtered, pieces = refs[0], refs[1:9]
    out, held_f, held_p, total, sem_f, sem_p = refs[9:]

    def f_copy(m):
        return pltpu.make_async_copy(filtered.at[groups[m]], held_f.at[m], sem_f.at[m])

    def p_copy(m):
        return pltpu.make_async_copy(
            pieces[m // 2].at[pl.ds(m % 2 * GROUP, GROUP)], held_p.at[m], sem_p.at[m]
        )

    for m in range(16):
        f_copy(m).start()
        p_copy(m).start()
    own = pltpu.make_async_copy(filtered.at[groups[16]], held_f.at[16], sem_f.at[16])
    own.start()
    total[...] = jnp.zeros_like(total)

    @pl.loop(0, 16)
    def _(m):
        f_copy(m).wait()
        pltpu.make_async_copy(
            pieces[0].at[pl.ds(0, GROUP)], held_p.at[m], sem_p.at[m]
        ).wait()
        base = groups[m] * 32
        for n in range(32):
            at = target[base + n] + n // 16 * GROUP
            total[at] += jnp.dot(
                held_f[m, n],
                held_p[m, inner_at[base + n]],
                preferred_element_type=jnp.float32,
            )

    own.wait()
    own_base = groups[16] * 32
    for n in range(32):
        at = inner_at[own_base + n] + n // 16 * GROUP
        total[at] += -1.5 * held_f[16, n].astype(jnp.float32)
    for i in range(2):
        for j in range(GROUP):
            out[i * B : (i + 1) * B, j * B : (j + 1) * B] = (
                -2.0 * total[i * GROUP + j]
            ).astype(jnp.bfloat16)


def cubed(groups, inner_at, target, filtered, pieces):
    return pl.pallas_call(
        cubed_kernel,
        grid_spec=pltpu.PrefetchScalarGridSpec(
            num_scalar_prefetch=3,
            grid=(),
            in_specs=[pl.BlockSpec(memory_space=pl.ANY)] * 9,
            out_specs=pl.BlockSpec(memory_space=pltpu.VMEM),
            scratch_shapes=[
                pltpu.VMEM((17, 32, B, B), jnp.bfloat16),
                pltpu.VMEM((16, GROUP, B, B), jnp.bfloat16),
                pltpu.VMEM((64, B, B), jnp.float32),
                pltpu.SemaphoreType.DMA((17,)),
                pltpu.SemaphoreType.DMA((16,)),
            ],
        ),
        out_shape=jax.ShapeDtypeStruct((2 * B, GROUP * B), jnp.bfloat16),
        compiler_params=pltpu.CompilerParams(vmem_limit_bytes=48 * MIB),
        cost_estimate=pl.CostEstimate(
            flops=4 * 512 * 2 * B**3, bytes_accessed=36 * MIB, transcendentals=0
        ),
        name="cubed",
    )(groups, inner_at, target, filtered, *pieces)


def is_equal(values, count):
    return values[..., None] == jnp.arange(count, dtype=jnp.int32)


def picked(values, table):
    return jnp.sum(jnp.where(is_equal(values, table.shape[0]), table, 0), axis=-1)


def local(owned_blocks, owned_rows, owned_cols, keep):
    r, c = lax.axis_index("row"), lax.axis_index("col")
    outgoing = owned_blocks.reshape(ROWS, 2, COLS, B, B).transpose(0, 2, 1, 3, 4)
    arrived = lax.all_to_all(
        outgoing.reshape(ROWS * COLS, 2, B, B), AXES, split_axis=0, concat_axis=0, tiled=True
    ).reshape(256, B, B)

    tags = jnp.concatenate([owned_cols.reshape(-1), owned_rows, jnp.zeros(752, jnp.int32)])
    tags = lax.all_to_all(
        jnp.broadcast_to(tags.reshape(1, 8, 128), (ROWS * COLS, 8, 128)),
        AXES,
        split_axis=0,
        concat_axis=0,
        tiled=True,
    )
    all_rows = tags[:, 2, :16]
    all_cols = tags[:, :2].reshape(2048, COLS)
    bands = (jnp.arange(16, dtype=jnp.int32) // 2)[None]
    ids = GROUP * (bands + ROWS * (all_rows // GROUP)) + all_rows % GROUP
    ids = jnp.where(all_rows < 64, ids, -1).reshape(2048)
    spots = (ids[None] == jnp.arange(512, dtype=jnp.int32)[:, None]).astype(jnp.bfloat16)
    cols = jnp.dot(
        spots, all_cols.astype(jnp.bfloat16), preferred_element_type=jnp.float32
    ).astype(jnp.int32)

    band_tags = lax.dynamic_slice_in_dim(all_rows, 2 * r, 2, 1).reshape(256)
    place = jnp.sum(
        jnp.where(
            band_tags[None] == jnp.arange(64, dtype=jnp.int32)[:, None],
            jnp.arange(256, dtype=jnp.int32)[None],
            0,
        ),
        axis=1,
    )
    window_cols = cols.reshape(16, GROUP, COLS)[:ROWS, :2]
    wanted = lax.dynamic_slice_in_dim(
        window_cols.reshape(ROWS, 2, 2, ROWS), r, 1, 3
    )[..., 0]
    wanted = wanted + GROUP * jnp.arange(2, dtype=jnp.int32)
    where = jnp.concatenate([place, picked(wanted.reshape(32), place)])

    mine = lax.dynamic_index_in_dim(window_cols, r, 0, keepdims=False)
    rows_in = (mine + GROUP * jnp.arange(COLS, dtype=jnp.int32)[None]).reshape(32)
    tcol = (
        jnp.dot(
            is_equal(rows_in, 512).astype(jnp.bfloat16),
            cols.astype(jnp.bfloat16),
            preferred_element_type=jnp.float32,
        )
        .astype(jnp.int32)
        .reshape(2, 16, COLS)
    )
    my_cols = lax.dynamic_slice_in_dim(cols, c, 1, 1).reshape(COLS, GROUP)
    inner_at = tcol.transpose(2, 0, 1)
    target = jnp.sum(
        jnp.where(is_equal(inner_at, GROUP), my_cols[:, None, None, :], 0), axis=-1
    )
    here = lax.dynamic_index_in_dim(inner_at, c, 0, keepdims=False)
    same = here[:, :, None] == here[:, None, :]
    order = jnp.arange(16, dtype=jnp.int32)
    leader = jnp.min(jnp.where(same, order, 16), axis=-1)
    kept = jnp.sum(jnp.where(is_equal(here, GROUP), keep[:, None, :], 0), axis=-1)
    mask = jnp.where(leader == order, kept, 0)

    band, inner, window = pack(where, arrived)

    pieces = {(0, 0): band}
    pieces[1, 0] = send_row(band, -1, 0)
    pieces[3, 0] = send_row(band, 1, 0)
    pieces[0, 1] = send_row(band, 0, 1)
    pieces[1, 1] = send_row(pieces[0, 1], -1, 0)
    pieces[3, 1] = send_row(pieces[0, 1], 1, 0)
    pieces[2, 0] = send_row(pieces[1, 0], -1, 0)
    pieces[2, 1] = send_row(pieces[3, 1], 1, 0)

    left = lax.all_gather(window, "col", axis=0, tiled=True).reshape(COLS, 2, B, B)
    inner = lax.all_to_all(
        inner.reshape(ROWS, 4, B, B), "row", split_axis=0, concat_axis=0, tiled=True
    ).reshape(ROWS, 2, 2, B, B)
    filtered = square(
        leader.reshape(32),
        mask.reshape(32),
        left,
        inner,
        [pieces[key] for key in ((1, 0), (3, 0), (0, 1))],
    )
    filtered = lax.all_gather(filtered[None], "col", axis=0, tiled=True)

    order = [(0, 0), (1, 0), (3, 0), (0, 1), (2, 0), (3, 1), (1, 1), (2, 1)]
    groups = []
    for dy, dz in order:
        band_id = (r // 2 + dy) % 4 * 2 + (r % 2 + dz) % 2
        groups += [band_id, band_id + ROWS]
    groups = jnp.stack(groups + [c]).astype(jnp.int32)
    return cubed(
        groups,
        inner_at.reshape(512),
        target.reshape(512),
        filtered,
        [pieces[key] for key in order],
    )


def solution(mesh):
    placed = (P(AXES, None, None, None), P(AXES), P(AXES, None), P("row", "col"))
    return jax.shard_map(
        local, mesh=mesh, in_specs=placed, out_specs=P("row", "col"), check_vma=False
    )
```

```python
import functools

import jax
import jax.numpy as jnp
from jax import lax
from jax.experimental import pallas as pl
from jax.experimental.pallas import tpu as pltpu
from jax.sharding import PartitionSpec as P

AXES = ("row", "col")
B = 128
ROWS, COLS = 8, 16
GROUP = 32
MIB = 1 << 20
ROOM = 63 * MIB
EARLY = ((0, 0), (0, 1), (1, 0), (1, 1), (3, 0), (3, 1), (2, 0))
LATE = ((2, 1),)


def moved(by_y, flip_z):
    pairs = []
    for r in range(ROWS):
        y, z = r // 2, r % 2
        pairs.append((r, (y + by_y) % 4 * 2 + (z ^ flip_z)))
    return pairs


def send_col(value, by_x, flip_z, flip_core):
    pairs = []
    for n in range(COLS):
        x, z, core = n // 4, n // 2 % 2, n % 2
        pairs.append((n, (x + by_x) % 4 * 4 + (z ^ flip_z) * 2 + (core ^ flip_core)))
    return lax.ppermute(value, "col", pairs)


def send_row(value, by_y, flip_z):
    return lax.ppermute(value, "row", moved(by_y, flip_z))


def spread_kernel(owned, blocks, held, sem_in, sem_out):
    def read(n):
        return pltpu.make_async_copy(
            owned.at[n], held.at[n // 2, :, n % 2], sem_in.at[n]
        )

    def write(h):
        return pltpu.make_async_copy(held.at[h], blocks.at[h], sem_out.at[h])

    for n in range(2 * ROWS):
        read(n).start()
    for h in range(ROWS):
        read(2 * h).wait()
        read(2 * h + 1).wait()
        write(h).start()
    for h in range(ROWS):
        write(h).wait()


def spread(owned):
    return pl.pallas_call(
        spread_kernel,
        in_specs=[pl.BlockSpec(memory_space=pl.ANY)],
        out_specs=pl.BlockSpec(memory_space=pl.ANY),
        scratch_shapes=[
            pltpu.VMEM((ROWS, COLS, 2, B, B), jnp.bfloat16),
            pltpu.SemaphoreType.DMA((2 * ROWS,)),
            pltpu.SemaphoreType.DMA((ROWS,)),
        ],
        out_shape=jax.ShapeDtypeStruct((ROWS, COLS, 2, B, B), jnp.bfloat16),
        compiler_params=pltpu.CompilerParams(vmem_limit_bytes=ROOM),
        cost_estimate=pl.CostEstimate(flops=0, bytes_accessed=16 * MIB, transcendentals=0),
        name="spread",
    )(owned)


def after_kernel(*refs):
    del refs


def after(values, others):
    return pl.pallas_call(
        after_kernel,
        in_specs=[pl.BlockSpec(memory_space=pltpu.HBM)] * (len(values) + len(others)),
        out_specs=[pl.BlockSpec(memory_space=pltpu.HBM)] * len(values),
        out_shape=[jax.ShapeDtypeStruct(v.shape, v.dtype) for v in values],
        input_output_aliases={n: n for n in range(len(values))},
        compiler_params=pltpu.CompilerParams(vmem_limit_bytes=ROOM),
        cost_estimate=pl.CostEstimate(flops=0, bytes_accessed=1024, transcendentals=0),
        name="after",
    )(*values, *others)


def pack_kernel(parts, where, arrived, *refs):
    outs, held, sem, sems = refs[-3 - parts : -3], *refs[-3:]
    count = held.shape[0]

    @pl.loop(0, count)
    def _(n):
        pltpu.make_async_copy(arrived.at[where[n]], held.at[n], sem).start()

    pltpu.make_async_copy(arrived.at[pl.ds(0, count)], held, sem).wait()
    size = count // parts
    writes = [
        pltpu.make_async_copy(held.at[pl.ds(n * size, size)], out, sems.at[n])
        for n, out in enumerate(outs)
    ]
    for write in writes:
        write.start()
    for write in writes:
        write.wait()


def pack(where, arrived, others=(), parts=1):
    count = where.shape[0]
    return pl.pallas_call(
        functools.partial(pack_kernel, parts),
        grid_spec=pltpu.PrefetchScalarGridSpec(
            num_scalar_prefetch=1,
            grid=(),
            in_specs=[pl.BlockSpec(memory_space=pltpu.HBM)] * (1 + len(others)),
            out_specs=[pl.BlockSpec(memory_space=pltpu.HBM)] * parts,
            scratch_shapes=[
                pltpu.VMEM((count, B, B), jnp.bfloat16),
                pltpu.SemaphoreType.DMA,
                pltpu.SemaphoreType.DMA((parts,)),
            ],
        ),
        out_shape=[jax.ShapeDtypeStruct((count // parts, B, B), jnp.bfloat16)] * parts,
        compiler_params=pltpu.CompilerParams(vmem_limit_bytes=ROOM),
        cost_estimate=pl.CostEstimate(
            flops=0, bytes_accessed=4 * count * B * B, transcendentals=0
        ),
        name="pack",
    )(where, arrived, *others)


def square_kernel(groups, leader, mask, left, *refs):
    out, held, done, total, sem_in, sem_out = refs[-6:]
    count = held.shape[0]

    def write(p):
        return pltpu.make_async_copy(done.at[p], out.at[p], sem_out.at[p])

    for p, inner in enumerate(refs[:count]):
        pltpu.make_async_copy(inner, held.at[p], sem_in.at[p]).start()

    @pl.loop(0, count)
    def _(p):
        pltpu.make_async_copy(refs[0], held.at[p], sem_in.at[p]).wait()
        base = groups[p] * 32
        total[...] = jnp.zeros_like(total)
        for g in range(COLS):
            for i in range(2):
                at = leader[base + i * 16 + g]
                total[i * 16 + at] += jnp.dot(
                    left[g, i],
                    held[p, g % ROWS * 4 + i * 2 + g // ROWS],
                    preferred_element_type=jnp.float32,
                )
        for n in range(32):
            kept = mask[base + n].astype(jnp.float32)
            done[p, n] = (total[n] * kept).astype(jnp.bfloat16)
        write(p).start()

    for p in range(count):
        write(p).wait()


def square(groups, leader, mask, left, inners, others):
    count = len(inners)
    hbm = pl.BlockSpec(memory_space=pltpu.HBM)
    return pl.pallas_call(
        square_kernel,
        grid_spec=pltpu.PrefetchScalarGridSpec(
            num_scalar_prefetch=3,
            grid=(),
            in_specs=[pl.BlockSpec(memory_space=pltpu.VMEM)]
            + [hbm] * (count + len(others)),
            out_specs=hbm,
            scratch_shapes=[
                pltpu.VMEM((count, 32, B, B), jnp.bfloat16),
                pltpu.VMEM((count, 32, B, B), jnp.bfloat16),
                pltpu.VMEM((32, B, B), jnp.float32),
                pltpu.SemaphoreType.DMA((count,)),
                pltpu.SemaphoreType.DMA((count,)),
            ],
        ),
        out_shape=jax.ShapeDtypeStruct((count, 32, B, B), jnp.bfloat16),
        compiler_params=pltpu.CompilerParams(vmem_limit_bytes=ROOM),
        cost_estimate=pl.CostEstimate(
            flops=count * 32 * 2 * B**3, bytes_accessed=2 * count * MIB, transcendentals=0
        ),
        name="square",
    )(groups, leader, mask, left, *inners, *others)


def cubed_kernel(is_last, groups, slots, inner_at, target, *refs):
    filtered, refs = refs[:4], refs[4:]
    count = len(refs) - 7
    pieces, (before, out, held_f, held_p, total, sem_f, sem_p) = refs[:count], refs[count:]
    steps, spare = held_f.shape[0] - 1, held_f.shape[0] - 1

    def f_start(m):
        place, core = slots[m] // 2, slots[m] % 2
        for n, blocks in enumerate(filtered):
            first = n // 2 * len(EARLY)
            found = (place >= first) & (place < first + blocks.shape[0])

            @pl.when(found & (core == n % 2))
            def _():
                pltpu.make_async_copy(
                    blocks.at[place - first], held_f.at[m], sem_f.at[m]
                ).start()

    def f_wait(m):
        pltpu.make_async_copy(filtered[0].at[0], held_f.at[m], sem_f.at[m]).wait()

    if is_last:
        last = pltpu.make_async_copy(before, total, sem_f.at[spare])
    else:
        last = pltpu.make_async_copy(filtered[0].at[0], held_f.at[spare], sem_f.at[spare])
    last.start()
    m = 0
    for piece in pieces:
        for first in range(0, piece.shape[0], GROUP):
            f_start(m)
            pltpu.make_async_copy(
                piece.at[pl.ds(first, GROUP)], held_p.at[m], sem_p.at[m]
            ).start()
            m += 1
    if is_last:
        last.wait()
    else:
        total[...] = jnp.zeros_like(total)

    @pl.loop(0, steps)
    def _(m):
        f_wait(m)
        pltpu.make_async_copy(
            pieces[0].at[pl.ds(0, GROUP)], held_p.at[m], sem_p.at[m]
        ).wait()
        base = groups[m] * 32
        for n in range(32):
            at = target[base + n] + n // 16 * GROUP
            total[at] += jnp.dot(
                held_f[m, n],
                held_p[m, inner_at[base + n]],
                preferred_element_type=jnp.float32,
            )

    if is_last:
        for i in range(2):
            for j in range(GROUP):
                out[i * B : (i + 1) * B, j * B : (j + 1) * B] = (
                    -2.0 * total[i * GROUP + j]
                ).astype(jnp.bfloat16)
    else:
        last.wait()
        own = groups[steps] * 32
        for n in range(32):
            at = inner_at[own + n] + n // 16 * GROUP
            total[at] += -1.5 * held_f[spare, n].astype(jnp.float32)
        copy = pltpu.make_async_copy(total, out, sem_f.at[spare])
        copy.start()
        copy.wait()


def cubed(groups, slots, inner_at, target, filtered, pieces, before):
    is_last = before is not None
    steps = sum(piece.shape[0] for piece in pieces) // GROUP
    if is_last:
        shape = jax.ShapeDtypeStruct((2 * B, GROUP * B), jnp.bfloat16)
        spec = pl.BlockSpec(memory_space=pltpu.VMEM)
    else:
        shape = jax.ShapeDtypeStruct((64, B, B), jnp.float32)
        spec = pl.BlockSpec(memory_space=pltpu.HBM)
        before = filtered[0]
    return pl.pallas_call(
        functools.partial(cubed_kernel, is_last),
        grid_spec=pltpu.PrefetchScalarGridSpec(
            num_scalar_prefetch=4,
            grid=(),
            in_specs=[pl.BlockSpec(memory_space=pltpu.HBM)] * (5 + len(pieces)),
            out_specs=spec,
            scratch_shapes=[
                pltpu.VMEM((steps + 1, 32, B, B), jnp.bfloat16),
                pltpu.VMEM((steps, GROUP, B, B), jnp.bfloat16),
                pltpu.VMEM((64, B, B), jnp.float32),
                pltpu.SemaphoreType.DMA((steps + 1,)),
                pltpu.SemaphoreType.DMA((steps,)),
            ],
        ),
        out_shape=shape,
        compiler_params=pltpu.CompilerParams(vmem_limit_bytes=ROOM),
        cost_estimate=pl.CostEstimate(
            flops=4 * steps * 32 * 2 * B**3,
            bytes_accessed=(2 * steps + 5) * MIB,
            transcendentals=0,
        ),
        name="cubed",
    )(groups, slots, inner_at, target, *filtered, *pieces, before)


def is_equal(values, count):
    return values[..., None] == jnp.arange(count, dtype=jnp.int32)


def picked(values, table):
    return jnp.sum(jnp.where(is_equal(values, table.shape[0]), table, 0), axis=-1)


def local(owned_blocks, owned_rows, owned_cols, keep):
    r, c = lax.axis_index("row"), lax.axis_index("col")
    tags = jnp.concatenate(
        [owned_cols.reshape(-1), owned_rows, keep.reshape(-1), jnp.zeros(688, jnp.int32)]
    )
    outgoing = spread(owned_blocks)
    arrived = lax.all_to_all(
        outgoing.reshape(ROWS * COLS, 2, B, B), AXES, split_axis=0, concat_axis=0, tiled=True
    ).reshape(256, B, B)

    tags = lax.all_to_all(
        jnp.broadcast_to(tags.reshape(1, 8, 128), (ROWS * COLS, 8, 128)),
        AXES,
        split_axis=0,
        concat_axis=0,
        tiled=True,
    )
    all_rows = tags[:, 2, :16]
    all_cols = tags[:, :2].reshape(2048, COLS)
    bands = (jnp.arange(16, dtype=jnp.int32) // 2)[None]
    ids = GROUP * (bands + ROWS * (all_rows // GROUP)) + all_rows % GROUP
    ids = jnp.where(all_rows < 64, ids, -1).reshape(2048)
    spots = (ids[None] == jnp.arange(512, dtype=jnp.int32)[:, None]).astype(jnp.bfloat16)
    cols = jnp.dot(
        spots, all_cols.astype(jnp.bfloat16), preferred_element_type=jnp.float32
    ).astype(jnp.int32)

    band_tags = lax.dynamic_slice_in_dim(all_rows, 2 * r, 2, 1).reshape(256)
    place = jnp.sum(
        jnp.where(
            band_tags[None] == jnp.arange(64, dtype=jnp.int32)[:, None],
            jnp.arange(256, dtype=jnp.int32)[None],
            0,
        ),
        axis=1,
    )
    window_cols = cols.reshape(16, GROUP, COLS)[:ROWS, :2]
    wanted = lax.dynamic_slice_in_dim(
        window_cols.reshape(ROWS, 2, 2, ROWS), r, 1, 3
    )[..., 0]
    wanted = wanted + GROUP * jnp.arange(2, dtype=jnp.int32)
    where = jnp.concatenate([picked(wanted.reshape(32), place), place[:2]])

    mine = lax.dynamic_index_in_dim(window_cols, r, 0, keepdims=False)
    rows_in = (mine + GROUP * jnp.arange(COLS, dtype=jnp.int32)[None]).reshape(32)
    tcol = (
        jnp.dot(
            is_equal(rows_in, 512).astype(jnp.bfloat16),
            cols.astype(jnp.bfloat16),
            preferred_element_type=jnp.float32,
        )
        .astype(jnp.int32)
        .reshape(2, 16, COLS)
    )
    my_cols = lax.dynamic_slice_in_dim(cols, c, 1, 1).reshape(COLS, GROUP)
    inner_at = tcol.transpose(2, 0, 1)
    target = jnp.sum(
        jnp.where(is_equal(inner_at, GROUP), my_cols[:, None, None, :], 0), axis=-1
    )
    same = inner_at[:, :, :, None] == inner_at[:, :, None, :]
    order = jnp.arange(16, dtype=jnp.int32)
    leader = jnp.min(jnp.where(same, order, 16), axis=-1)
    keep = lax.dynamic_slice_in_dim(tags[:, 2, 16:80], r * COLS, COLS, 0)
    keep = keep.reshape(COLS, 2, 1, GROUP)
    kept = jnp.sum(jnp.where(is_equal(inner_at, GROUP), keep, 0), axis=-1)
    mask = jnp.where(leader == order, kept, 0)
    leader, mask = leader.reshape(512), mask.reshape(512)

    inner, window = pack(where[:32], arrived)[0], pack(where[32:], arrived)[0]
    band = pack(place, arrived, [inner, window], 2)
    left = lax.all_gather(window, "col", axis=0, tiled=True).reshape(COLS, 2, B, B)
    inner = lax.all_to_all(
        inner.reshape(ROWS, 4, B, B), "row", split_axis=0, concat_axis=0, tiled=True
    ).reshape(32, B, B)

    p, f = {(0, 0, 0): band[0]}, {}
    p[1, 0, 0] = send_row(band[0], -1, 0)
    p[3, 0, 0] = send_row(band[0], 1, 0)
    p[0, 1, 0] = send_row(band[0], 0, 1)
    f[1, 0] = send_col(inner, -1, 0, 0)
    f[3, 0] = send_col(inner, 1, 0, 0)

    keys = [(1, 0, 0), (3, 0, 0), (0, 1, 0)]
    second, f[0, 0], f[1, 0], f[3, 0], *held = after(
        [band[1], inner, f[1, 0], f[3, 0]] + [p[key] for key in keys], []
    )
    p.update(zip(keys, held))
    p[1, 0, 1] = send_row(second, -1, 0)
    p[3, 0, 1] = send_row(second, 1, 0)
    f[0, 1] = send_col(f[0, 0], 0, 1, 0)
    f[2, 0] = send_col(f[1, 0], -1, 0, 0)

    p[0, 0, 1], p[1, 0, 0], p[3, 0, 1], f[0, 1], f[2, 0] = after(
        [second, p[1, 0, 0], p[3, 0, 1], f[0, 1], f[2, 0]], [p[1, 0, 1]]
    )
    p[2, 0, 0] = send_row(p[1, 0, 0], -1, 0)
    p[2, 0, 1] = send_row(p[3, 0, 1], 1, 0)
    p[0, 1, 1] = send_row(p[0, 0, 1], 0, 1)
    f[1, 1] = send_col(f[0, 1], -1, 0, 0)
    f[3, 1] = send_col(f[0, 1], 1, 0, 0)

    p[0, 1, 0], p[2, 0, 0], f[3, 1], f[1, 1] = after(
        [p[0, 1, 0], p[2, 0, 0], f[3, 1], f[1, 1]], [p[2, 0, 1], p[0, 1, 1]]
    )
    p[1, 1, 0] = send_row(p[0, 1, 0], -1, 0)
    p[3, 1, 0] = send_row(p[0, 1, 0], 1, 0)
    p[2, 1, 0] = send_row(p[2, 0, 0], 0, 1)
    f[2, 1] = send_col(f[3, 1], 1, 0, 0)

    def squares(keys, others):
        ids = [(c // 4 + dx) % 4 * 4 + ((c % 4) ^ (2 * dz)) for dx, dz in keys]
        ids = jnp.stack(ids).astype(jnp.int32)
        return square(ids, leader, mask, left, [f[key] for key in keys], others)

    early, p[0, 1, 1], p[2, 0, 1], f[2, 1] = after(
        [squares(EARLY, []), p[0, 1, 1], p[2, 0, 1], f[2, 1]],
        [p[1, 1, 0], p[3, 1, 0], p[2, 1, 0]],
    )
    p[1, 1, 1] = send_row(p[0, 1, 1], -1, 0)
    p[3, 1, 1] = send_row(p[0, 1, 1], 1, 0)
    p[2, 1, 1] = send_row(p[2, 0, 1], 0, 1)
    filtered = [early, send_col(early, 0, 0, 1)]
    late = squares(LATE, [])
    filtered += [late, send_col(late, 0, 0, 1)]

    def products(keys, before):
        groups, slots = [], []
        for dy, dz, half in keys:
            group = (r // 2 + dy) % 4 * 2 + (r % 2 + dz) % 2 + ROWS * half
            groups.append(group)
            dx = (group // 4 - c // 4) % 4
            slots.append((dx ^ (dx // 2)) * 4 + ((group % 4) ^ (c % 4)))
        return cubed(
            jnp.stack(groups + [c]).astype(jnp.int32),
            jnp.stack(slots).astype(jnp.int32),
            inner_at.reshape(512),
            target.reshape(512),
            filtered,
            [p[key] for key in keys],
            before,
        )

    last = [(1, 1, 1), (3, 1, 1), (2, 1, 1)]
    total = products([key for key in p if key not in last], None)
    return products(last, total)


def solution(mesh):
    placed = (P(AXES, None, None, None), P(AXES), P(AXES, None), P("row", "col"))
    return jax.shard_map(
        local, mesh=mesh, in_specs=placed, out_specs=P("row", "col"), check_vma=False
    )
```

```python
import functools

import jax
import jax.numpy as jnp
from jax import lax
from jax.experimental import pallas as pl
from jax.experimental.pallas import tpu as pltpu
from jax.sharding import PartitionSpec as P

AXES = ("row", "col")
B = 128
ROWS, COLS = 8, 16
GROUP = 32
MIB = 1 << 20
ROOM = 63 * MIB
EARLY = ((0, 0), (0, 1), (1, 0), (1, 1), (3, 0), (3, 1), (2, 0))
LATE = (2, 1)


def moved(by_y, flip_z):
    pairs = []
    for r in range(ROWS):
        y, z = r // 2, r % 2
        pairs.append((r, (y + by_y) % 4 * 2 + (z ^ flip_z)))
    return pairs


def send_col(value, by_x, flip_z, flip_core):
    pairs = []
    for n in range(COLS):
        x, z, core = n // 4, n // 2 % 2, n % 2
        pairs.append((n, (x + by_x) % 4 * 4 + (z ^ flip_z) * 2 + (core ^ flip_core)))
    return lax.ppermute(value, "col", pairs)


def send_row(value, by_y, flip_z):
    return lax.ppermute(value, "row", moved(by_y, flip_z))


def spread_kernel(owned, blocks, held, sem_in, sem_out):
    def read(n):
        return pltpu.make_async_copy(
            owned.at[n], held.at[n // 2, :, n % 2], sem_in.at[n]
        )

    def write(h):
        return pltpu.make_async_copy(held.at[h], blocks.at[h], sem_out.at[h])

    for n in range(2 * ROWS):
        read(n).start()
    for h in range(ROWS):
        read(2 * h).wait()
        read(2 * h + 1).wait()
        write(h).start()
    for h in range(ROWS):
        write(h).wait()


def spread(owned):
    return pl.pallas_call(
        spread_kernel,
        in_specs=[pl.BlockSpec(memory_space=pl.ANY)],
        out_specs=pl.BlockSpec(memory_space=pl.ANY),
        scratch_shapes=[
            pltpu.VMEM((ROWS, COLS, 2, B, B), jnp.bfloat16),
            pltpu.SemaphoreType.DMA((2 * ROWS,)),
            pltpu.SemaphoreType.DMA((ROWS,)),
        ],
        out_shape=jax.ShapeDtypeStruct((ROWS, COLS, 2, B, B), jnp.bfloat16),
        compiler_params=pltpu.CompilerParams(vmem_limit_bytes=ROOM),
        cost_estimate=pl.CostEstimate(flops=0, bytes_accessed=16 * MIB, transcendentals=0),
        name="spread",
    )(owned)


def after_kernel(*refs):
    del refs


def after(values, others):
    return pl.pallas_call(
        after_kernel,
        in_specs=[pl.BlockSpec(memory_space=pltpu.HBM)] * (len(values) + len(others)),
        out_specs=[pl.BlockSpec(memory_space=pltpu.HBM)] * len(values),
        out_shape=[jax.ShapeDtypeStruct(v.shape, v.dtype) for v in values],
        input_output_aliases={n: n for n in range(len(values))},
        compiler_params=pltpu.CompilerParams(vmem_limit_bytes=ROOM),
        cost_estimate=pl.CostEstimate(flops=0, bytes_accessed=1024, transcendentals=0),
        name="after",
    )(*values, *others)


def pack_kernel(parts, where, arrived, *refs):
    outs, held, sem, sems = refs[-3 - parts : -3], *refs[-3:]
    count = held.shape[0]

    @pl.loop(0, count)
    def _(n):
        pltpu.make_async_copy(arrived.at[where[n]], held.at[n], sem).start()

    pltpu.make_async_copy(arrived.at[pl.ds(0, count)], held, sem).wait()
    size = count // parts
    writes = [
        pltpu.make_async_copy(held.at[pl.ds(n * size, size)], out, sems.at[n])
        for n, out in enumerate(outs)
    ]
    for write in writes:
        write.start()
    for write in writes:
        write.wait()


def pack(where, arrived, others=(), parts=1):
    count = where.shape[0]
    return pl.pallas_call(
        functools.partial(pack_kernel, parts),
        grid_spec=pltpu.PrefetchScalarGridSpec(
            num_scalar_prefetch=1,
            grid=(),
            in_specs=[pl.BlockSpec(memory_space=pltpu.HBM)] * (1 + len(others)),
            out_specs=[pl.BlockSpec(memory_space=pltpu.HBM)] * parts,
            scratch_shapes=[
                pltpu.VMEM((count, B, B), jnp.bfloat16),
                pltpu.SemaphoreType.DMA,
                pltpu.SemaphoreType.DMA((parts,)),
            ],
        ),
        out_shape=[jax.ShapeDtypeStruct((count // parts, B, B), jnp.bfloat16)] * parts,
        compiler_params=pltpu.CompilerParams(vmem_limit_bytes=ROOM),
        cost_estimate=pl.CostEstimate(
            flops=0, bytes_accessed=4 * count * B * B, transcendentals=0
        ),
        name="pack",
    )(where, arrived, *others)


def square_kernel(groups, leader, mask, left, *refs):
    out, held, done, total, sem_in, sem_out = refs[-6:]
    count = held.shape[0]

    def write(p):
        return pltpu.make_async_copy(done.at[p], out.at[p], sem_out.at[p])

    for p, inner in enumerate(refs[:count]):
        pltpu.make_async_copy(inner, held.at[p], sem_in.at[p]).start()

    @pl.loop(0, count)
    def _(p):
        pltpu.make_async_copy(refs[0], held.at[p], sem_in.at[p]).wait()
        base = groups[p] * 32
        total[...] = jnp.zeros_like(total)
        for g in range(COLS):
            for i in range(2):
                at = leader[base + i * 16 + g]
                total[i * 16 + at] += jnp.dot(
                    left[g, i],
                    held[p, g % ROWS * 4 + i * 2 + g // ROWS],
                    preferred_element_type=jnp.float32,
                )
        for n in range(32):
            kept = mask[base + n].astype(jnp.float32)
            done[p, n] = (total[n] * kept).astype(jnp.bfloat16)
        write(p).start()

    for p in range(count):
        write(p).wait()


def square(groups, leader, mask, left, inners, others):
    count = len(inners)
    hbm = pl.BlockSpec(memory_space=pltpu.HBM)
    return pl.pallas_call(
        square_kernel,
        grid_spec=pltpu.PrefetchScalarGridSpec(
            num_scalar_prefetch=3,
            grid=(),
            in_specs=[pl.BlockSpec(memory_space=pltpu.VMEM)]
            + [hbm] * (count + len(others)),
            out_specs=hbm,
            scratch_shapes=[
                pltpu.VMEM((count, 32, B, B), jnp.bfloat16),
                pltpu.VMEM((count, 32, B, B), jnp.bfloat16),
                pltpu.VMEM((32, B, B), jnp.float32),
                pltpu.SemaphoreType.DMA((count,)),
                pltpu.SemaphoreType.DMA((count,)),
            ],
        ),
        out_shape=jax.ShapeDtypeStruct((count, 32, B, B), jnp.bfloat16),
        compiler_params=pltpu.CompilerParams(vmem_limit_bytes=ROOM),
        cost_estimate=pl.CostEstimate(
            flops=count * 32 * 2 * B**3, bytes_accessed=2 * count * MIB, transcendentals=0
        ),
        name="square",
    )(groups, leader, mask, left, *inners, *others)


def cubed_kernel(is_last, groups, slots, inner_at, target, *refs):
    filtered, refs = refs[:3], refs[3:]
    count = len(refs) - 7
    pieces, (before, out, held_f, held_p, total, sem_f, sem_p) = refs[:count], refs[count:]
    steps, spare = held_f.shape[0] - 1, held_f.shape[0] - 1

    def f_start(m):
        place, core = slots[m] // 2, slots[m] % 2
        late = place == len(EARLY)
        for n, blocks in enumerate(filtered):
            found = late if n == 2 else (core == n) & ~late
            where = core if n == 2 else place

            @pl.when(found)
            def _():
                pltpu.make_async_copy(
                    blocks.at[where], held_f.at[m], sem_f.at[m]
                ).start()

    def f_wait(m):
        pltpu.make_async_copy(filtered[0].at[0], held_f.at[m], sem_f.at[m]).wait()

    if is_last:
        last = pltpu.make_async_copy(before, total, sem_f.at[spare])
    else:
        last = pltpu.make_async_copy(filtered[0].at[0], held_f.at[spare], sem_f.at[spare])
    last.start()
    m = 0
    for piece in pieces:
        for first in range(0, piece.shape[0], GROUP):
            f_start(m)
            pltpu.make_async_copy(
                piece.at[pl.ds(first, GROUP)], held_p.at[m], sem_p.at[m]
            ).start()
            m += 1
    if is_last:
        last.wait()
    else:
        total[...] = jnp.zeros_like(total)

    @pl.loop(0, steps)
    def _(m):
        f_wait(m)
        pltpu.make_async_copy(
            pieces[0].at[pl.ds(0, GROUP)], held_p.at[m], sem_p.at[m]
        ).wait()
        base = groups[m] * 32
        for n in range(32):
            at = target[base + n] + n // 16 * GROUP
            total[at] += jnp.dot(
                held_f[m, n],
                held_p[m, inner_at[base + n]],
                preferred_element_type=jnp.float32,
            )

    if is_last:
        for i in range(2):
            for j in range(GROUP):
                out[i * B : (i + 1) * B, j * B : (j + 1) * B] = (
                    -2.0 * total[i * GROUP + j]
                ).astype(jnp.bfloat16)
    else:
        last.wait()
        own = groups[steps] * 32
        for n in range(32):
            at = inner_at[own + n] + n // 16 * GROUP
            total[at] += -1.5 * held_f[spare, n].astype(jnp.float32)
        copy = pltpu.make_async_copy(total, out, sem_f.at[spare])
        copy.start()
        copy.wait()


def cubed(groups, slots, inner_at, target, filtered, pieces, before):
    is_last = before is not None
    steps = sum(piece.shape[0] for piece in pieces) // GROUP
    if is_last:
        shape = jax.ShapeDtypeStruct((2 * B, GROUP * B), jnp.bfloat16)
        spec = pl.BlockSpec(memory_space=pltpu.VMEM)
    else:
        shape = jax.ShapeDtypeStruct((64, B, B), jnp.float32)
        spec = pl.BlockSpec(memory_space=pltpu.HBM)
        before = filtered[0]
    return pl.pallas_call(
        functools.partial(cubed_kernel, is_last),
        grid_spec=pltpu.PrefetchScalarGridSpec(
            num_scalar_prefetch=4,
            grid=(),
            in_specs=[pl.BlockSpec(memory_space=pltpu.HBM)] * (4 + len(pieces)),
            out_specs=spec,
            scratch_shapes=[
                pltpu.VMEM((steps + 1, 32, B, B), jnp.bfloat16),
                pltpu.VMEM((steps, GROUP, B, B), jnp.bfloat16),
                pltpu.VMEM((64, B, B), jnp.float32),
                pltpu.SemaphoreType.DMA((steps + 1,)),
                pltpu.SemaphoreType.DMA((steps,)),
            ],
        ),
        out_shape=shape,
        compiler_params=pltpu.CompilerParams(vmem_limit_bytes=ROOM),
        cost_estimate=pl.CostEstimate(
            flops=4 * steps * 32 * 2 * B**3,
            bytes_accessed=(2 * steps + 5) * MIB,
            transcendentals=0,
        ),
        name="cubed",
    )(groups, slots, inner_at, target, *filtered, *pieces, before)


def is_equal(values, count):
    return values[..., None] == jnp.arange(count, dtype=jnp.int32)


def picked(values, table):
    return jnp.sum(jnp.where(is_equal(values, table.shape[0]), table, 0), axis=-1)


def local(owned_blocks, owned_rows, owned_cols, keep):
    r, c = lax.axis_index("row"), lax.axis_index("col")
    tags = jnp.concatenate(
        [owned_cols.reshape(-1), owned_rows, keep.reshape(-1), jnp.zeros(688, jnp.int32)]
    )
    outgoing = spread(owned_blocks)
    arrived = lax.all_to_all(
        outgoing.reshape(ROWS * COLS, 2, B, B), AXES, split_axis=0, concat_axis=0, tiled=True
    ).reshape(256, B, B)

    tags = lax.all_to_all(
        jnp.broadcast_to(tags.reshape(1, 8, 128), (ROWS * COLS, 8, 128)),
        AXES,
        split_axis=0,
        concat_axis=0,
        tiled=True,
    )
    all_rows = tags[:, 2, :16]
    all_cols = tags[:, :2].reshape(2048, COLS)
    bands = (jnp.arange(16, dtype=jnp.int32) // 2)[None]
    ids = GROUP * (bands + ROWS * (all_rows // GROUP)) + all_rows % GROUP
    ids = jnp.where(all_rows < 64, ids, -1).reshape(2048)
    spots = (ids[None] == jnp.arange(512, dtype=jnp.int32)[:, None]).astype(jnp.bfloat16)
    cols = jnp.dot(
        spots, all_cols.astype(jnp.bfloat16), preferred_element_type=jnp.float32
    ).astype(jnp.int32)

    band_tags = lax.dynamic_slice_in_dim(all_rows, 2 * r, 2, 1).reshape(256)
    place = jnp.sum(
        jnp.where(
            band_tags[None] == jnp.arange(64, dtype=jnp.int32)[:, None],
            jnp.arange(256, dtype=jnp.int32)[None],
            0,
        ),
        axis=1,
    )
    window_cols = cols.reshape(16, GROUP, COLS)[:ROWS, :2]
    wanted = lax.dynamic_slice_in_dim(
        window_cols.reshape(ROWS, 2, 2, ROWS), r, 1, 3
    )[..., 0]
    wanted = wanted + GROUP * jnp.arange(2, dtype=jnp.int32)
    where = jnp.concatenate([picked(wanted.reshape(32), place), place[:2]])

    mine = lax.dynamic_index_in_dim(window_cols, r, 0, keepdims=False)
    rows_in = (mine + GROUP * jnp.arange(COLS, dtype=jnp.int32)[None]).reshape(32)
    tcol = (
        jnp.dot(
            is_equal(rows_in, 512).astype(jnp.bfloat16),
            cols.astype(jnp.bfloat16),
            preferred_element_type=jnp.float32,
        )
        .astype(jnp.int32)
        .reshape(2, 16, COLS)
    )
    my_cols = lax.dynamic_slice_in_dim(cols, c, 1, 1).reshape(COLS, GROUP)
    inner_at = tcol.transpose(2, 0, 1)
    target = jnp.sum(
        jnp.where(is_equal(inner_at, GROUP), my_cols[:, None, None, :], 0), axis=-1
    )
    same = inner_at[:, :, :, None] == inner_at[:, :, None, :]
    order = jnp.arange(16, dtype=jnp.int32)
    leader = jnp.min(jnp.where(same, order, 16), axis=-1)
    keep = lax.dynamic_slice_in_dim(tags[:, 2, 16:80], r * COLS, COLS, 0)
    keep = keep.reshape(COLS, 2, 1, GROUP)
    kept = jnp.sum(jnp.where(is_equal(inner_at, GROUP), keep, 0), axis=-1)
    mask = jnp.where(leader == order, kept, 0)
    leader, mask = leader.reshape(512), mask.reshape(512)

    inner, window = pack(where[:32], arrived)[0], pack(where[32:], arrived)[0]
    band = pack(place, arrived, [inner], 2)
    left = lax.all_gather(window, "col", axis=0, tiled=True).reshape(COLS, 2, B, B)
    inner = lax.all_to_all(
        inner.reshape(ROWS, 4, B, B), "row", split_axis=0, concat_axis=0, tiled=True
    ).reshape(32, B, B)

    p, f = {(0, 0, 0): band[0]}, {}
    p[1, 0, 0] = send_row(band[0], -1, 0)
    p[3, 0, 0] = send_row(band[0], 1, 0)
    p[0, 1, 0] = send_row(band[0], 0, 1)
    f[1, 0] = send_col(inner, -1, 0, 0)
    f[3, 0] = send_col(inner, 1, 0, 0)

    keys = [(1, 0, 0), (3, 0, 0), (0, 1, 0)]
    second, *held = after([band[1]] + [p[key] for key in keys], [])
    p.update(zip(keys, held))
    p[1, 0, 1] = send_row(second, -1, 0)
    p[3, 0, 1] = send_row(second, 1, 0)
    f[0, 0] = inner
    f[0, 1] = send_col(inner, 0, 1, 0)
    f[2, 0] = send_col(f[1, 0], -1, 0, 0)

    p[0, 0, 1], p[1, 0, 0], p[3, 0, 1], f[0, 1], f[2, 0], f[3, 0] = after(
        [second, p[1, 0, 0], p[3, 0, 1], f[0, 1], f[2, 0], f[3, 0]], [p[1, 0, 1]]
    )
    p[2, 0, 0] = send_row(p[1, 0, 0], -1, 0)
    p[2, 0, 1] = send_row(p[3, 0, 1], 1, 0)
    p[0, 1, 1] = send_row(p[0, 0, 1], 0, 1)
    f[1, 1] = send_col(f[0, 1], -1, 0, 0)
    f[3, 1] = send_col(f[0, 1], 1, 0, 0)

    p[0, 1, 0], p[2, 0, 0], f[3, 1], f[1, 1] = after(
        [p[0, 1, 0], p[2, 0, 0], f[3, 1], f[1, 1]], [p[2, 0, 1], p[0, 1, 1]]
    )
    p[1, 1, 0] = send_row(p[0, 1, 0], -1, 0)
    p[3, 1, 0] = send_row(p[0, 1, 0], 1, 0)
    p[2, 1, 0] = send_row(p[2, 0, 0], 0, 1)
    f[2, 1] = send_col(f[3, 1], 1, 0, 0)

    def squares(blocks):
        ids = [
            (c // 4 + dx) % 4 * 4 + ((c % 4) ^ (2 * dz + core)) for dx, dz, core in blocks
        ]
        ids = jnp.stack(ids).astype(jnp.int32)
        return square(ids, leader, mask, left, list(blocks.values()), [])

    early, p[0, 1, 1], p[2, 0, 1], f[2, 1] = after(
        [squares({(*key, 0): f[key] for key in EARLY}), p[0, 1, 1], p[2, 0, 1], f[2, 1]],
        [p[1, 1, 0], p[3, 1, 0], p[2, 1, 0]],
    )
    p[1, 1, 1] = send_row(p[0, 1, 1], -1, 0)
    p[3, 1, 1] = send_row(p[0, 1, 1], 1, 0)
    p[2, 1, 1] = send_row(p[2, 0, 1], 0, 1)
    other = send_col(f[LATE], 0, 0, 1)
    late = squares({(*LATE, 0): f[LATE], (*LATE, 1): other})
    filtered = [early, send_col(early, 0, 0, 1), late]

    def products(keys, before):
        groups, slots = [], []
        for dy, dz, half in keys:
            group = (r // 2 + dy) % 4 * 2 + (r % 2 + dz) % 2 + ROWS * half
            groups.append(group)
            dx = (group // 4 - c // 4) % 4
            slots.append((dx ^ (dx // 2)) * 4 + ((group % 4) ^ (c % 4)))
        return cubed(
            jnp.stack(groups + [c]).astype(jnp.int32),
            jnp.stack(slots).astype(jnp.int32),
            inner_at.reshape(512),
            target.reshape(512),
            filtered,
            [p[key] for key in keys],
            before,
        )

    last = [(1, 1, 1), (3, 1, 1), (2, 1, 1)]
    total = products([key for key in p if key not in last], None)
    return products(last, total)


def solution(mesh):
    placed = (P(AXES, None, None, None), P(AXES), P(AXES, None), P("row", "col"))
    return jax.shard_map(
        local, mesh=mesh, in_specs=placed, out_specs=P("row", "col"), check_vma=False
    )
```

```python
import functools

import jax
import jax.numpy as jnp
from jax import lax
from jax.experimental import pallas as pl
from jax.experimental.pallas import tpu as pltpu
from jax.sharding import PartitionSpec as P

AXES = ("row", "col")
B = 128
ROWS, COLS = 8, 16
GROUP = 32
MIB = 1 << 20
ROOM = 63 * MIB
EARLY = ((0, 0), (0, 1), (1, 0), (1, 1), (3, 0), (3, 1))
LATE = ((2, 0), (2, 1))


def moved(by_y, flip_z):
    pairs = []
    for r in range(ROWS):
        y, z = r // 2, r % 2
        pairs.append((r, (y + by_y) % 4 * 2 + (z ^ flip_z)))
    return pairs


def send_col(value, by_x, flip_z, flip_core):
    pairs = []
    for n in range(COLS):
        x, z, core = n // 4, n // 2 % 2, n % 2
        pairs.append((n, (x + by_x) % 4 * 4 + (z ^ flip_z) * 2 + (core ^ flip_core)))
    return lax.ppermute(value, "col", pairs)


def send_row(value, by_y, flip_z):
    return lax.ppermute(value, "row", moved(by_y, flip_z))


def spread_kernel(owned, blocks, held, sem_in, sem_out):
    def read(n):
        return pltpu.make_async_copy(
            owned.at[n], held.at[n // 2, :, n % 2], sem_in.at[n]
        )

    def write(h):
        return pltpu.make_async_copy(held.at[h], blocks.at[h], sem_out.at[h])

    for n in range(2 * ROWS):
        read(n).start()
    for h in range(ROWS):
        read(2 * h).wait()
        read(2 * h + 1).wait()
        write(h).start()
    for h in range(ROWS):
        write(h).wait()


def spread(owned):
    return pl.pallas_call(
        spread_kernel,
        in_specs=[pl.BlockSpec(memory_space=pl.ANY)],
        out_specs=pl.BlockSpec(memory_space=pl.ANY),
        scratch_shapes=[
            pltpu.VMEM((ROWS, COLS, 2, B, B), jnp.bfloat16),
            pltpu.SemaphoreType.DMA((2 * ROWS,)),
            pltpu.SemaphoreType.DMA((ROWS,)),
        ],
        out_shape=jax.ShapeDtypeStruct((ROWS, COLS, 2, B, B), jnp.bfloat16),
        compiler_params=pltpu.CompilerParams(vmem_limit_bytes=ROOM),
        cost_estimate=pl.CostEstimate(flops=0, bytes_accessed=16 * MIB, transcendentals=0),
        name="spread",
    )(owned)


def after_kernel(*refs):
    del refs


def after(values, others):
    return pl.pallas_call(
        after_kernel,
        in_specs=[pl.BlockSpec(memory_space=pltpu.HBM)] * (len(values) + len(others)),
        out_specs=[pl.BlockSpec(memory_space=pltpu.HBM)] * len(values),
        out_shape=[jax.ShapeDtypeStruct(v.shape, v.dtype) for v in values],
        input_output_aliases={n: n for n in range(len(values))},
        compiler_params=pltpu.CompilerParams(vmem_limit_bytes=ROOM),
        cost_estimate=pl.CostEstimate(flops=0, bytes_accessed=1024, transcendentals=0),
        name="after",
    )(*values, *others)


def pack_kernel(parts, where, arrived, *refs):
    outs, held, sem, sems = refs[-3 - parts : -3], *refs[-3:]
    count = held.shape[0]

    @pl.loop(0, count)
    def _(n):
        pltpu.make_async_copy(arrived.at[where[n]], held.at[n], sem).start()

    pltpu.make_async_copy(arrived.at[pl.ds(0, count)], held, sem).wait()
    size = count // parts
    writes = [
        pltpu.make_async_copy(held.at[pl.ds(n * size, size)], out, sems.at[n])
        for n, out in enumerate(outs)
    ]
    for write in writes:
        write.start()
    for write in writes:
        write.wait()


def pack(where, arrived, others=(), parts=1):
    count = where.shape[0]
    return pl.pallas_call(
        functools.partial(pack_kernel, parts),
        grid_spec=pltpu.PrefetchScalarGridSpec(
            num_scalar_prefetch=1,
            grid=(),
            in_specs=[pl.BlockSpec(memory_space=pltpu.HBM)] * (1 + len(others)),
            out_specs=[pl.BlockSpec(memory_space=pltpu.HBM)] * parts,
            scratch_shapes=[
                pltpu.VMEM((count, B, B), jnp.bfloat16),
                pltpu.SemaphoreType.DMA,
                pltpu.SemaphoreType.DMA((parts,)),
            ],
        ),
        out_shape=[jax.ShapeDtypeStruct((count // parts, B, B), jnp.bfloat16)] * parts,
        compiler_params=pltpu.CompilerParams(vmem_limit_bytes=ROOM),
        cost_estimate=pl.CostEstimate(
            flops=0, bytes_accessed=4 * count * B * B, transcendentals=0
        ),
        name="pack",
    )(where, arrived, *others)


def square_kernel(groups, leader, mask, left, *refs):
    out, held, done, total, sem_in, sem_out = refs[-6:]
    count = held.shape[0]

    def write(p):
        return pltpu.make_async_copy(done.at[p], out.at[p], sem_out.at[p])

    for p, inner in enumerate(refs[:count]):
        pltpu.make_async_copy(inner, held.at[p], sem_in.at[p]).start()

    @pl.loop(0, count)
    def _(p):
        pltpu.make_async_copy(refs[0], held.at[p], sem_in.at[p]).wait()
        base = groups[p] * 32
        total[...] = jnp.zeros_like(total)
        for g in range(COLS):
            for i in range(2):
                at = leader[base + i * 16 + g]
                total[i * 16 + at] += jnp.dot(
                    left[g, i],
                    held[p, g % ROWS * 4 + i * 2 + g // ROWS],
                    preferred_element_type=jnp.float32,
                )
        for n in range(32):
            kept = mask[base + n].astype(jnp.float32)
            done[p, n] = (total[n] * kept).astype(jnp.bfloat16)
        write(p).start()

    for p in range(count):
        write(p).wait()


def square(groups, leader, mask, left, inners, others):
    count = len(inners)
    hbm = pl.BlockSpec(memory_space=pltpu.HBM)
    return pl.pallas_call(
        square_kernel,
        grid_spec=pltpu.PrefetchScalarGridSpec(
            num_scalar_prefetch=3,
            grid=(),
            in_specs=[pl.BlockSpec(memory_space=pltpu.VMEM)]
            + [hbm] * (count + len(others)),
            out_specs=hbm,
            scratch_shapes=[
                pltpu.VMEM((count, 32, B, B), jnp.bfloat16),
                pltpu.VMEM((count, 32, B, B), jnp.bfloat16),
                pltpu.VMEM((32, B, B), jnp.float32),
                pltpu.SemaphoreType.DMA((count,)),
                pltpu.SemaphoreType.DMA((count,)),
            ],
        ),
        out_shape=jax.ShapeDtypeStruct((count, 32, B, B), jnp.bfloat16),
        compiler_params=pltpu.CompilerParams(vmem_limit_bytes=ROOM),
        cost_estimate=pl.CostEstimate(
            flops=count * 32 * 2 * B**3, bytes_accessed=2 * count * MIB, transcendentals=0
        ),
        name="square",
    )(groups, leader, mask, left, *inners, *others)


def cubed_kernel(is_last, groups, slots, inner_at, target, *refs):
    filtered, refs = refs[:4], refs[4:]
    count = len(refs) - 7
    pieces, (before, out, held_f, held_p, total, sem_f, sem_p) = refs[:count], refs[count:]
    steps, spare = held_f.shape[0] - 1, held_f.shape[0] - 1

    def f_start(m):
        place, core = slots[m] // 2, slots[m] % 2
        for n, blocks in enumerate(filtered):
            first = n // 2 * len(EARLY)
            found = (place >= first) & (place < first + blocks.shape[0])

            @pl.when(found & (core == n % 2))
            def _():
                pltpu.make_async_copy(
                    blocks.at[place - first], held_f.at[m], sem_f.at[m]
                ).start()

    def f_wait(m):
        pltpu.make_async_copy(filtered[0].at[0], held_f.at[m], sem_f.at[m]).wait()

    if is_last:
        last = pltpu.make_async_copy(before, total, sem_f.at[spare])
    else:
        last = pltpu.make_async_copy(filtered[0].at[0], held_f.at[spare], sem_f.at[spare])
    last.start()
    m = 0
    for piece in pieces:
        for first in range(0, piece.shape[0], GROUP):
            f_start(m)
            pltpu.make_async_copy(
                piece.at[pl.ds(first, GROUP)], held_p.at[m], sem_p.at[m]
            ).start()
            m += 1
    if is_last:
        last.wait()
    else:
        total[...] = jnp.zeros_like(total)

    @pl.loop(0, steps)
    def _(m):
        f_wait(m)
        pltpu.make_async_copy(
            pieces[0].at[pl.ds(0, GROUP)], held_p.at[m], sem_p.at[m]
        ).wait()
        base = groups[m] * 32
        for n in range(32):
            at = target[base + n] + n // 16 * GROUP
            total[at] += jnp.dot(
                held_f[m, n],
                held_p[m, inner_at[base + n]],
                preferred_element_type=jnp.float32,
            )

    if is_last:
        for i in range(2):
            for j in range(GROUP):
                out[i * B : (i + 1) * B, j * B : (j + 1) * B] = (
                    -2.0 * total[i * GROUP + j]
                ).astype(jnp.bfloat16)
    else:
        last.wait()
        own = groups[steps] * 32
        for n in range(32):
            at = inner_at[own + n] + n // 16 * GROUP
            total[at] += -1.5 * held_f[spare, n].astype(jnp.float32)
        copy = pltpu.make_async_copy(total, out, sem_f.at[spare])
        copy.start()
        copy.wait()


def cubed(groups, slots, inner_at, target, filtered, pieces, before):
    is_last = before is not None
    steps = sum(piece.shape[0] for piece in pieces) // GROUP
    if is_last:
        shape = jax.ShapeDtypeStruct((2 * B, GROUP * B), jnp.bfloat16)
        spec = pl.BlockSpec(memory_space=pltpu.VMEM)
    else:
        shape = jax.ShapeDtypeStruct((64, B, B), jnp.float32)
        spec = pl.BlockSpec(memory_space=pltpu.HBM)
        before = filtered[0]
    return pl.pallas_call(
        functools.partial(cubed_kernel, is_last),
        grid_spec=pltpu.PrefetchScalarGridSpec(
            num_scalar_prefetch=4,
            grid=(),
            in_specs=[pl.BlockSpec(memory_space=pltpu.HBM)] * (5 + len(pieces)),
            out_specs=spec,
            scratch_shapes=[
                pltpu.VMEM((steps + 1, 32, B, B), jnp.bfloat16),
                pltpu.VMEM((steps, GROUP, B, B), jnp.bfloat16),
                pltpu.VMEM((64, B, B), jnp.float32),
                pltpu.SemaphoreType.DMA((steps + 1,)),
                pltpu.SemaphoreType.DMA((steps,)),
            ],
        ),
        out_shape=shape,
        compiler_params=pltpu.CompilerParams(vmem_limit_bytes=ROOM),
        cost_estimate=pl.CostEstimate(
            flops=4 * steps * 32 * 2 * B**3,
            bytes_accessed=(2 * steps + 5) * MIB,
            transcendentals=0,
        ),
        name="cubed",
    )(groups, slots, inner_at, target, *filtered, *pieces, before)


def is_equal(values, count):
    return values[..., None] == jnp.arange(count, dtype=jnp.int32)


def picked(values, table):
    return jnp.sum(jnp.where(is_equal(values, table.shape[0]), table, 0), axis=-1)


def local(owned_blocks, owned_rows, owned_cols, keep):
    r, c = lax.axis_index("row"), lax.axis_index("col")
    tags = jnp.concatenate(
        [owned_cols.reshape(-1), owned_rows, keep.reshape(-1), jnp.zeros(688, jnp.int32)]
    )
    outgoing = spread(owned_blocks)
    arrived = lax.all_to_all(
        outgoing.reshape(ROWS * COLS, 2, B, B), AXES, split_axis=0, concat_axis=0, tiled=True
    ).reshape(256, B, B)

    tags = lax.all_to_all(
        jnp.broadcast_to(tags.reshape(1, 8, 128), (ROWS * COLS, 8, 128)),
        AXES,
        split_axis=0,
        concat_axis=0,
        tiled=True,
    )
    all_rows = tags[:, 2, :16]
    all_cols = tags[:, :2].reshape(2048, COLS)
    bands = (jnp.arange(16, dtype=jnp.int32) // 2)[None]
    ids = GROUP * (bands + ROWS * (all_rows // GROUP)) + all_rows % GROUP
    ids = jnp.where(all_rows < 64, ids, -1).reshape(2048)
    spots = (ids[None] == jnp.arange(512, dtype=jnp.int32)[:, None]).astype(jnp.bfloat16)
    cols = jnp.dot(
        spots, all_cols.astype(jnp.bfloat16), preferred_element_type=jnp.float32
    ).astype(jnp.int32)

    band_tags = lax.dynamic_slice_in_dim(all_rows, 2 * r, 2, 1).reshape(256)
    place = jnp.sum(
        jnp.where(
            band_tags[None] == jnp.arange(64, dtype=jnp.int32)[:, None],
            jnp.arange(256, dtype=jnp.int32)[None],
            0,
        ),
        axis=1,
    )
    window_cols = cols.reshape(16, GROUP, COLS)[:ROWS, :2]
    wanted = lax.dynamic_slice_in_dim(
        window_cols.reshape(ROWS, 2, 2, ROWS), r, 1, 3
    )[..., 0]
    wanted = wanted + GROUP * jnp.arange(2, dtype=jnp.int32)
    where = jnp.concatenate([picked(wanted.reshape(32), place), place[:2]])

    mine = lax.dynamic_index_in_dim(window_cols, r, 0, keepdims=False)
    rows_in = (mine + GROUP * jnp.arange(COLS, dtype=jnp.int32)[None]).reshape(32)
    tcol = (
        jnp.dot(
            is_equal(rows_in, 512).astype(jnp.bfloat16),
            cols.astype(jnp.bfloat16),
            preferred_element_type=jnp.float32,
        )
        .astype(jnp.int32)
        .reshape(2, 16, COLS)
    )
    my_cols = lax.dynamic_slice_in_dim(cols, c, 1, 1).reshape(COLS, GROUP)
    inner_at = tcol.transpose(2, 0, 1)
    target = jnp.sum(
        jnp.where(is_equal(inner_at, GROUP), my_cols[:, None, None, :], 0), axis=-1
    )
    same = inner_at[:, :, :, None] == inner_at[:, :, None, :]
    order = jnp.arange(16, dtype=jnp.int32)
    leader = jnp.min(jnp.where(same, order, 16), axis=-1)
    keep = lax.dynamic_slice_in_dim(tags[:, 2, 16:80], r * COLS, COLS, 0)
    keep = keep.reshape(COLS, 2, 1, GROUP)
    kept = jnp.sum(jnp.where(is_equal(inner_at, GROUP), keep, 0), axis=-1)
    mask = jnp.where(leader == order, kept, 0)
    leader, mask = leader.reshape(512), mask.reshape(512)

    inner, window = pack(where[:32], arrived)[0], pack(where[32:], arrived)[0]
    band = pack(place, arrived, [inner], 2)
    left = lax.all_gather(window, "col", axis=0, tiled=True).reshape(COLS, 2, B, B)
    inner = lax.all_to_all(
        inner.reshape(ROWS, 4, B, B), "row", split_axis=0, concat_axis=0, tiled=True
    ).reshape(32, B, B)

    p, f = {}, {(0, 0): inner}
    p[1, 0, 0] = send_row(band[0], -1, 0)
    p[3, 0, 0] = send_row(band[0], 1, 0)
    f[1, 0] = send_col(inner, -1, 0, 0)
    f[3, 0] = send_col(inner, 1, 0, 0)
    f[0, 1] = send_col(inner, 0, 1, 0)

    p[0, 0, 0], second, p[1, 0, 0], p[3, 0, 0] = after(
        [*band, p[1, 0, 0], p[3, 0, 0]], []
    )
    p[1, 0, 1] = send_row(second, -1, 0)
    p[3, 0, 1] = send_row(second, 1, 0)
    p[0, 1, 0] = send_row(p[0, 0, 0], 0, 1)
    f[1, 1] = send_col(f[0, 1], -1, 0, 0)
    f[3, 1] = send_col(f[0, 1], 1, 0, 0)

    keys = [(1, 0), (3, 0), (1, 1), (3, 1)]
    p[0, 0, 1], p[1, 0, 0], p[3, 0, 1], p[0, 1, 0], *held = after(
        [second, p[1, 0, 0], p[3, 0, 1], p[0, 1, 0]] + [f[key] for key in keys],
        [p[1, 0, 1]],
    )
    f.update(zip(keys, held))
    p[2, 0, 0] = send_row(p[1, 0, 0], -1, 0)
    p[2, 0, 1] = send_row(p[3, 0, 1], 1, 0)
    p[0, 1, 1] = send_row(p[0, 0, 1], 0, 1)
    f[2, 0] = send_col(f[1, 0], -1, 0, 0)
    f[2, 1] = send_col(f[3, 1], 1, 0, 0)

    def squares(keys):
        ids = [(c // 4 + dx) % 4 * 4 + ((c % 4) ^ (2 * dz)) for dx, dz in keys]
        ids = jnp.stack(ids).astype(jnp.int32)
        return square(ids, leader, mask, left, [f[key] for key in keys], [])

    keys = [(0, 1, 0), (0, 1, 1), (2, 0, 0), (2, 0, 1)]
    early, f[2, 0], f[2, 1], *held = after(
        [squares(EARLY), f[2, 0], f[2, 1]] + [p[key] for key in keys], []
    )
    p.update(zip(keys, held))
    p[1, 1, 0] = send_row(p[0, 1, 0], -1, 0)
    p[3, 1, 0] = send_row(p[0, 1, 0], 1, 0)
    p[2, 1, 0] = send_row(p[2, 0, 0], 0, 1)
    filtered = [early, send_col(early, 0, 0, 1)]

    late, p[0, 1, 1], p[2, 0, 1] = after(
        [squares(LATE), p[0, 1, 1], p[2, 0, 1]],
        [p[1, 1, 0], p[3, 1, 0], p[2, 1, 0]],
    )
    p[1, 1, 1] = send_row(p[0, 1, 1], -1, 0)
    p[3, 1, 1] = send_row(p[0, 1, 1], 1, 0)
    p[2, 1, 1] = send_row(p[2, 0, 1], 0, 1)
    filtered += [late, send_col(late, 0, 0, 1)]

    def products(keys, before):
        groups, slots = [], []
        for dy, dz, half in keys:
            group = (r // 2 + dy) % 4 * 2 + (r % 2 + dz) % 2 + ROWS * half
            groups.append(group)
            dx = (group // 4 - c // 4) % 4
            slots.append((dx ^ (dx // 2)) * 4 + ((group % 4) ^ (c % 4)))
        return cubed(
            jnp.stack(groups + [c]).astype(jnp.int32),
            jnp.stack(slots).astype(jnp.int32),
            inner_at.reshape(512),
            target.reshape(512),
            filtered,
            [p[key] for key in keys],
            before,
        )

    last = [(1, 1, 1), (3, 1, 1), (2, 1, 1)]
    total = products([key for key in p if key not in last], None)
    return products(last, total)


def solution(mesh):
    placed = (P(AXES, None, None, None), P(AXES), P(AXES, None), P("row", "col"))
    return jax.shard_map(
        local, mesh=mesh, in_specs=placed, out_specs=P("row", "col"), check_vma=False
    )
```

```python
import functools

import jax
import jax.numpy as jnp
from jax import lax
from jax.experimental import pallas as pl
from jax.experimental.pallas import tpu as pltpu
from jax.sharding import PartitionSpec as P

AXES = ("row", "col")
B = 128
ROWS, COLS = 8, 16
GROUP = 32
MIB = 1 << 20
ROOM = 63 * MIB
EARLY = ((0, 0), (0, 1), (1, 0), (1, 1), (3, 0), (3, 1))
LATE = ((2, 0), (2, 1))


def moved(by_y, flip_z):
    pairs = []
    for r in range(ROWS):
        y, z = r // 2, r % 2
        pairs.append((r, (y + by_y) % 4 * 2 + (z ^ flip_z)))
    return pairs


def send_col(value, by_x, flip_z, flip_core):
    pairs = []
    for n in range(COLS):
        x, z, core = n // 4, n // 2 % 2, n % 2
        pairs.append((n, (x + by_x) % 4 * 4 + (z ^ flip_z) * 2 + (core ^ flip_core)))
    return lax.ppermute(value, "col", pairs)


def send_row(value, by_y, flip_z):
    return lax.ppermute(value, "row", moved(by_y, flip_z))


def spread_kernel(owned, blocks, held, sem_in, sem_out):
    def read(n):
        return pltpu.make_async_copy(
            owned.at[n], held.at[n // 2, :, n % 2], sem_in.at[n]
        )

    def write(h):
        return pltpu.make_async_copy(held.at[h], blocks.at[h], sem_out.at[h])

    for n in range(2 * ROWS):
        read(n).start()
    for h in range(ROWS):
        read(2 * h).wait()
        read(2 * h + 1).wait()
        write(h).start()
    for h in range(ROWS):
        write(h).wait()


def spread(owned):
    return pl.pallas_call(
        spread_kernel,
        in_specs=[pl.BlockSpec(memory_space=pl.ANY)],
        out_specs=pl.BlockSpec(memory_space=pl.ANY),
        scratch_shapes=[
            pltpu.VMEM((ROWS, COLS, 2, B, B), jnp.bfloat16),
            pltpu.SemaphoreType.DMA((2 * ROWS,)),
            pltpu.SemaphoreType.DMA((ROWS,)),
        ],
        out_shape=jax.ShapeDtypeStruct((ROWS, COLS, 2, B, B), jnp.bfloat16),
        compiler_params=pltpu.CompilerParams(vmem_limit_bytes=ROOM),
        cost_estimate=pl.CostEstimate(flops=0, bytes_accessed=16 * MIB, transcendentals=0),
        name="spread",
    )(owned)


def after_kernel(*refs):
    del refs


def after(values, others):
    return pl.pallas_call(
        after_kernel,
        in_specs=[pl.BlockSpec(memory_space=pltpu.HBM)] * (len(values) + len(others)),
        out_specs=[pl.BlockSpec(memory_space=pltpu.HBM)] * len(values),
        out_shape=[jax.ShapeDtypeStruct(v.shape, v.dtype) for v in values],
        input_output_aliases={n: n for n in range(len(values))},
        compiler_params=pltpu.CompilerParams(vmem_limit_bytes=ROOM),
        cost_estimate=pl.CostEstimate(flops=0, bytes_accessed=1024, transcendentals=0),
        name="after",
    )(*values, *others)


def pack_kernel(parts, where, arrived, *refs):
    outs, held, sem, sems = refs[-3 - parts : -3], *refs[-3:]
    count = held.shape[0]

    @pl.loop(0, count)
    def _(n):
        pltpu.make_async_copy(arrived.at[where[n]], held.at[n], sem).start()

    pltpu.make_async_copy(arrived.at[pl.ds(0, count)], held, sem).wait()
    size = count // parts
    writes = [
        pltpu.make_async_copy(held.at[pl.ds(n * size, size)], out, sems.at[n])
        for n, out in enumerate(outs)
    ]
    for write in writes:
        write.start()
    for write in writes:
        write.wait()


def pack(where, arrived, others=(), parts=1):
    count = where.shape[0]
    return pl.pallas_call(
        functools.partial(pack_kernel, parts),
        grid_spec=pltpu.PrefetchScalarGridSpec(
            num_scalar_prefetch=1,
            grid=(),
            in_specs=[pl.BlockSpec(memory_space=pltpu.HBM)] * (1 + len(others)),
            out_specs=[pl.BlockSpec(memory_space=pltpu.HBM)] * parts,
            scratch_shapes=[
                pltpu.VMEM((count, B, B), jnp.bfloat16),
                pltpu.SemaphoreType.DMA,
                pltpu.SemaphoreType.DMA((parts,)),
            ],
        ),
        out_shape=[jax.ShapeDtypeStruct((count // parts, B, B), jnp.bfloat16)] * parts,
        compiler_params=pltpu.CompilerParams(vmem_limit_bytes=ROOM),
        cost_estimate=pl.CostEstimate(
            flops=0, bytes_accessed=4 * count * B * B, transcendentals=0
        ),
        name="pack",
    )(where, arrived, *others)


def square_kernel(groups, leader, mask, left, *refs):
    out, held, done, total, sem_in, sem_out = refs[-6:]
    count = held.shape[0]

    def write(p):
        return pltpu.make_async_copy(done.at[p], out.at[p], sem_out.at[p])

    for p, inner in enumerate(refs[:count]):
        pltpu.make_async_copy(inner, held.at[p], sem_in.at[p]).start()

    @pl.loop(0, count)
    def _(p):
        pltpu.make_async_copy(refs[0], held.at[p], sem_in.at[p]).wait()
        base = groups[p] * 32
        total[...] = jnp.zeros_like(total)
        for g in range(COLS):
            for i in range(2):
                at = leader[base + i * 16 + g]
                total[i * 16 + at] += jnp.dot(
                    left[g, i],
                    held[p, g % ROWS * 4 + i * 2 + g // ROWS],
                    preferred_element_type=jnp.float32,
                )
        for n in range(32):
            kept = mask[base + n].astype(jnp.float32)
            done[p, n] = (total[n] * kept).astype(jnp.bfloat16)
        write(p).start()

    for p in range(count):
        write(p).wait()


def square(groups, leader, mask, left, inners, others):
    count = len(inners)
    hbm = pl.BlockSpec(memory_space=pltpu.HBM)
    return pl.pallas_call(
        square_kernel,
        grid_spec=pltpu.PrefetchScalarGridSpec(
            num_scalar_prefetch=3,
            grid=(),
            in_specs=[pl.BlockSpec(memory_space=pltpu.VMEM)]
            + [hbm] * (count + len(others)),
            out_specs=hbm,
            scratch_shapes=[
                pltpu.VMEM((count, 32, B, B), jnp.bfloat16),
                pltpu.VMEM((count, 32, B, B), jnp.bfloat16),
                pltpu.VMEM((32, B, B), jnp.float32),
                pltpu.SemaphoreType.DMA((count,)),
                pltpu.SemaphoreType.DMA((count,)),
            ],
        ),
        out_shape=jax.ShapeDtypeStruct((count, 32, B, B), jnp.bfloat16),
        compiler_params=pltpu.CompilerParams(vmem_limit_bytes=ROOM),
        cost_estimate=pl.CostEstimate(
            flops=count * 32 * 2 * B**3, bytes_accessed=2 * count * MIB, transcendentals=0
        ),
        name="square",
    )(groups, leader, mask, left, *inners, *others)


def cubed_kernel(is_last, groups, slots, inner_at, target, *refs):
    filtered, refs = refs[:4], refs[4:]
    count = len(refs) - 7
    pieces, (before, out, held_f, held_p, total, sem_f, sem_p) = refs[:count], refs[count:]
    steps, spare = held_f.shape[0] - 1, held_f.shape[0] - 1

    def f_start(m):
        place, core = slots[m] // 2, slots[m] % 2
        for n, blocks in enumerate(filtered):
            first = n // 2 * len(EARLY)
            found = (place >= first) & (place < first + blocks.shape[0])

            @pl.when(found & (core == n % 2))
            def _():
                pltpu.make_async_copy(
                    blocks.at[place - first], held_f.at[m], sem_f.at[m]
                ).start()

    def f_wait(m):
        pltpu.make_async_copy(filtered[0].at[0], held_f.at[m], sem_f.at[m]).wait()

    if is_last:
        last = pltpu.make_async_copy(before, total, sem_f.at[spare])
    else:
        last = pltpu.make_async_copy(filtered[0].at[0], held_f.at[spare], sem_f.at[spare])
    last.start()
    m = 0
    for piece in pieces:
        for first in range(0, piece.shape[0], GROUP):
            f_start(m)
            pltpu.make_async_copy(
                piece.at[pl.ds(first, GROUP)], held_p.at[m], sem_p.at[m]
            ).start()
            m += 1
    if is_last:
        last.wait()
    else:
        total[...] = jnp.zeros_like(total)

    @pl.loop(0, steps)
    def _(m):
        f_wait(m)
        pltpu.make_async_copy(
            pieces[0].at[pl.ds(0, GROUP)], held_p.at[m], sem_p.at[m]
        ).wait()
        base = groups[m] * 32
        for n in range(32):
            at = target[base + n] + n // 16 * GROUP
            total[at] += jnp.dot(
                held_f[m, n],
                held_p[m, inner_at[base + n]],
                preferred_element_type=jnp.float32,
            )

    if is_last:
        for i in range(2):
            for j in range(GROUP):
                out[i * B : (i + 1) * B, j * B : (j + 1) * B] = (
                    -2.0 * total[i * GROUP + j]
                ).astype(jnp.bfloat16)
    else:
        last.wait()
        own = groups[steps] * 32
        for n in range(32):
            at = inner_at[own + n] + n // 16 * GROUP
            total[at] += -1.5 * held_f[spare, n].astype(jnp.float32)
        copy = pltpu.make_async_copy(total, out, sem_f.at[spare])
        copy.start()
        copy.wait()


def cubed(groups, slots, inner_at, target, filtered, pieces, before):
    is_last = before is not None
    steps = sum(piece.shape[0] for piece in pieces) // GROUP
    if is_last:
        shape = jax.ShapeDtypeStruct((2 * B, GROUP * B), jnp.bfloat16)
        spec = pl.BlockSpec(memory_space=pltpu.VMEM)
    else:
        shape = jax.ShapeDtypeStruct((64, B, B), jnp.float32)
        spec = pl.BlockSpec(memory_space=pltpu.HBM)
        before = filtered[0]
    return pl.pallas_call(
        functools.partial(cubed_kernel, is_last),
        grid_spec=pltpu.PrefetchScalarGridSpec(
            num_scalar_prefetch=4,
            grid=(),
            in_specs=[pl.BlockSpec(memory_space=pltpu.HBM)] * (5 + len(pieces)),
            out_specs=spec,
            scratch_shapes=[
                pltpu.VMEM((steps + 1, 32, B, B), jnp.bfloat16),
                pltpu.VMEM((steps, GROUP, B, B), jnp.bfloat16),
                pltpu.VMEM((64, B, B), jnp.float32),
                pltpu.SemaphoreType.DMA((steps + 1,)),
                pltpu.SemaphoreType.DMA((steps,)),
            ],
        ),
        out_shape=shape,
        compiler_params=pltpu.CompilerParams(vmem_limit_bytes=ROOM),
        cost_estimate=pl.CostEstimate(
            flops=4 * steps * 32 * 2 * B**3,
            bytes_accessed=(2 * steps + 5) * MIB,
            transcendentals=0,
        ),
        name="cubed",
    )(groups, slots, inner_at, target, *filtered, *pieces, before)


def is_equal(values, count):
    return values[..., None] == jnp.arange(count, dtype=jnp.int32)


def picked(values, table):
    return jnp.sum(jnp.where(is_equal(values, table.shape[0]), table, 0), axis=-1)


def local(owned_blocks, owned_rows, owned_cols, keep):
    r, c = lax.axis_index("row"), lax.axis_index("col")
    tags = jnp.concatenate(
        [owned_cols.reshape(-1), owned_rows, keep.reshape(-1), jnp.zeros(688, jnp.int32)]
    )
    outgoing = spread(owned_blocks)
    arrived = lax.all_to_all(
        outgoing.reshape(ROWS * COLS, 2, B, B), AXES, split_axis=0, concat_axis=0, tiled=True
    ).reshape(256, B, B)

    tags = lax.all_to_all(
        jnp.broadcast_to(tags.reshape(1, 8, 128), (ROWS * COLS, 8, 128)),
        AXES,
        split_axis=0,
        concat_axis=0,
        tiled=True,
    )
    all_rows = tags[:, 2, :16]
    all_cols = tags[:, :2].reshape(2048, COLS)
    bands = (jnp.arange(16, dtype=jnp.int32) // 2)[None]
    ids = GROUP * (bands + ROWS * (all_rows // GROUP)) + all_rows % GROUP
    ids = jnp.where(all_rows < 64, ids, -1).reshape(2048)
    spots = (ids[None] == jnp.arange(512, dtype=jnp.int32)[:, None]).astype(jnp.bfloat16)
    cols = jnp.dot(
        spots, all_cols.astype(jnp.bfloat16), preferred_element_type=jnp.float32
    ).astype(jnp.int32)

    band_tags = lax.dynamic_slice_in_dim(all_rows, 2 * r, 2, 1).reshape(256)
    place = jnp.sum(
        jnp.where(
            band_tags[None] == jnp.arange(64, dtype=jnp.int32)[:, None],
            jnp.arange(256, dtype=jnp.int32)[None],
            0,
        ),
        axis=1,
    )
    window_cols = cols.reshape(16, GROUP, COLS)[:ROWS, :2]
    wanted = lax.dynamic_slice_in_dim(
        window_cols.reshape(ROWS, 2, 2, ROWS), r, 1, 3
    )[..., 0]
    wanted = wanted + GROUP * jnp.arange(2, dtype=jnp.int32)
    where = jnp.concatenate([picked(wanted.reshape(32), place), place[:2]])

    mine = lax.dynamic_index_in_dim(window_cols, r, 0, keepdims=False)
    rows_in = (mine + GROUP * jnp.arange(COLS, dtype=jnp.int32)[None]).reshape(32)
    tcol = (
        jnp.dot(
            is_equal(rows_in, 512).astype(jnp.bfloat16),
            cols.astype(jnp.bfloat16),
            preferred_element_type=jnp.float32,
        )
        .astype(jnp.int32)
        .reshape(2, 16, COLS)
    )
    my_cols = lax.dynamic_slice_in_dim(cols, c, 1, 1).reshape(COLS, GROUP)
    inner_at = tcol.transpose(2, 0, 1)
    target = jnp.sum(
        jnp.where(is_equal(inner_at, GROUP), my_cols[:, None, None, :], 0), axis=-1
    )
    same = inner_at[:, :, :, None] == inner_at[:, :, None, :]
    order = jnp.arange(16, dtype=jnp.int32)
    leader = jnp.min(jnp.where(same, order, 16), axis=-1)
    keep = lax.dynamic_slice_in_dim(tags[:, 2, 16:80], r * COLS, COLS, 0)
    keep = keep.reshape(COLS, 2, 1, GROUP)
    kept = jnp.sum(jnp.where(is_equal(inner_at, GROUP), keep, 0), axis=-1)
    mask = jnp.where(leader == order, kept, 0)
    leader, mask = leader.reshape(512), mask.reshape(512)

    inner, window = pack(where[:32], arrived)[0], pack(where[32:], arrived)[0]
    band = pack(place, arrived, [inner], 2)
    left = lax.all_gather(window, "col", axis=0, tiled=True).reshape(COLS, 2, B, B)
    inner = lax.all_to_all(
        inner.reshape(ROWS, 4, B, B), "row", split_axis=0, concat_axis=0, tiled=True
    ).reshape(32, B, B)

    p, f = {}, {(0, 0): inner}
    p[1, 0, 0] = send_row(band[0], -1, 0)
    p[3, 0, 0] = send_row(band[0], 1, 0)
    f[1, 0] = send_col(inner, -1, 0, 0)
    f[3, 0] = send_col(inner, 1, 0, 0)
    f[0, 1] = send_col(inner, 0, 1, 0)

    p[0, 0, 0], second, p[1, 0, 0], p[3, 0, 0] = after(
        [*band, p[1, 0, 0], p[3, 0, 0]], []
    )
    p[1, 0, 1] = send_row(second, -1, 0)
    p[3, 0, 1] = send_row(second, 1, 0)
    p[0, 1, 0] = send_row(p[0, 0, 0], 0, 1)
    f[1, 1] = send_col(f[0, 1], -1, 0, 0)
    f[3, 1] = send_col(f[0, 1], 1, 0, 0)

    p[0, 0, 1], p[1, 0, 0], p[3, 0, 1], p[0, 1, 0], f[1, 0], f[3, 0] = after(
        [second, p[1, 0, 0], p[3, 0, 1], p[0, 1, 0], f[1, 0], f[3, 0]],
        [p[1, 0, 1], f[0, 1]],
    )
    p[2, 0, 0] = send_row(p[1, 0, 0], -1, 0)
    p[2, 0, 1] = send_row(p[3, 0, 1], 1, 0)
    p[0, 1, 1] = send_row(p[0, 0, 1], 0, 1)

    f[1, 0], f[3, 1] = after([f[1, 0], f[3, 1]], [f[1, 1], p[0, 0, 1]])
    f[2, 0] = send_col(f[1, 0], -1, 0, 0)
    f[2, 1] = send_col(f[3, 1], 1, 0, 0)

    keys = [(0, 1, 0), (0, 1, 1), (2, 0, 0), (2, 0, 1)]
    p.update(zip(keys, after([p[key] for key in keys], [])))
    p[1, 1, 0] = send_row(p[0, 1, 0], -1, 0)
    p[3, 1, 0] = send_row(p[0, 1, 0], 1, 0)
    p[2, 1, 0] = send_row(p[2, 0, 0], 0, 1)

    def squares(keys):
        ids = [(c // 4 + dx) % 4 * 4 + ((c % 4) ^ (2 * dz)) for dx, dz in keys]
        ids = jnp.stack(ids).astype(jnp.int32)
        return square(ids, leader, mask, left, [f[key] for key in keys], [])

    early, late, p[0, 1, 1], p[2, 0, 1] = after(
        [squares(EARLY), squares(LATE), p[0, 1, 1], p[2, 0, 1]],
        [p[1, 1, 0], p[3, 1, 0], p[2, 1, 0]],
    )
    p[1, 1, 1] = send_row(p[0, 1, 1], -1, 0)
    p[3, 1, 1] = send_row(p[0, 1, 1], 1, 0)
    p[2, 1, 1] = send_row(p[2, 0, 1], 0, 1)
    filtered = [early, send_col(early, 0, 0, 1), late, send_col(late, 0, 0, 1)]

    def products(keys, before):
        groups, slots = [], []
        for dy, dz, half in keys:
            group = (r // 2 + dy) % 4 * 2 + (r % 2 + dz) % 2 + ROWS * half
            groups.append(group)
            dx = (group // 4 - c // 4) % 4
            slots.append((dx ^ (dx // 2)) * 4 + ((group % 4) ^ (c % 4)))
        return cubed(
            jnp.stack(groups + [c]).astype(jnp.int32),
            jnp.stack(slots).astype(jnp.int32),
            inner_at.reshape(512),
            target.reshape(512),
            filtered,
            [p[key] for key in keys],
            before,
        )

    last = [(1, 1, 1), (3, 1, 1), (2, 1, 1)]
    total = products([key for key in p if key not in last], None)
    return products(last, total)


def solution(mesh):
    placed = (P(AXES, None, None, None), P(AXES), P(AXES, None), P("row", "col"))
    return jax.shard_map(
        local, mesh=mesh, in_specs=placed, out_specs=P("row", "col"), check_vma=False
    )
```

```python
import functools

import jax
import jax.numpy as jnp
from jax import lax
from jax.experimental import pallas as pl
from jax.experimental.pallas import tpu as pltpu
from jax.sharding import PartitionSpec as P

AXES = ("row", "col")
B = 128
ROWS, COLS = 8, 16
GROUP = 32
MIB = 1 << 20
ROOM = 63 * MIB
EARLY = ((0, 0), (0, 1), (1, 0), (1, 1), (3, 0), (3, 1))
LATE = ((2, 0), (2, 1))


def moved(by_y, flip_z):
    pairs = []
    for r in range(ROWS):
        y, z = r // 2, r % 2
        pairs.append((r, (y + by_y) % 4 * 2 + (z ^ flip_z)))
    return pairs


def send_col(value, by_x, flip_z, flip_core):
    pairs = []
    for n in range(COLS):
        x, z, core = n // 4, n // 2 % 2, n % 2
        pairs.append((n, (x + by_x) % 4 * 4 + (z ^ flip_z) * 2 + (core ^ flip_core)))
    return lax.ppermute(value, "col", pairs)


def send_row(value, by_y, flip_z):
    return lax.ppermute(value, "row", moved(by_y, flip_z))


def spread_kernel(owned, blocks, held, sem_in, sem_out):
    def read(n):
        return pltpu.make_async_copy(
            owned.at[n], held.at[n // 2, :, n % 2], sem_in.at[n]
        )

    def write(h):
        return pltpu.make_async_copy(held.at[h], blocks.at[h], sem_out.at[h])

    for n in range(2 * ROWS):
        read(n).start()
    for h in range(ROWS):
        read(2 * h).wait()
        read(2 * h + 1).wait()
        write(h).start()
    for h in range(ROWS):
        write(h).wait()


def spread(owned):
    return pl.pallas_call(
        spread_kernel,
        in_specs=[pl.BlockSpec(memory_space=pl.ANY)],
        out_specs=pl.BlockSpec(memory_space=pl.ANY),
        scratch_shapes=[
            pltpu.VMEM((ROWS, COLS, 2, B, B), jnp.bfloat16),
            pltpu.SemaphoreType.DMA((2 * ROWS,)),
            pltpu.SemaphoreType.DMA((ROWS,)),
        ],
        out_shape=jax.ShapeDtypeStruct((ROWS, COLS, 2, B, B), jnp.bfloat16),
        compiler_params=pltpu.CompilerParams(vmem_limit_bytes=ROOM),
        cost_estimate=pl.CostEstimate(flops=0, bytes_accessed=16 * MIB, transcendentals=0),
        name="spread",
    )(owned)


def after_kernel(*refs):
    del refs


def after(values, others):
    return pl.pallas_call(
        after_kernel,
        in_specs=[pl.BlockSpec(memory_space=pltpu.HBM)] * (len(values) + len(others)),
        out_specs=[pl.BlockSpec(memory_space=pltpu.HBM)] * len(values),
        out_shape=[jax.ShapeDtypeStruct(v.shape, v.dtype) for v in values],
        input_output_aliases={n: n for n in range(len(values))},
        compiler_params=pltpu.CompilerParams(vmem_limit_bytes=ROOM),
        cost_estimate=pl.CostEstimate(flops=0, bytes_accessed=1024, transcendentals=0),
        name="after",
    )(*values, *others)


def pack_kernel(parts, where, arrived, *refs):
    outs, held, sem, sems = refs[-3 - parts : -3], *refs[-3:]
    count = held.shape[0]

    @pl.loop(0, count)
    def _(n):
        pltpu.make_async_copy(arrived.at[where[n]], held.at[n], sem).start()

    pltpu.make_async_copy(arrived.at[pl.ds(0, count)], held, sem).wait()
    size = count // parts
    writes = [
        pltpu.make_async_copy(held.at[pl.ds(n * size, size)], out, sems.at[n])
        for n, out in enumerate(outs)
    ]
    for write in writes:
        write.start()
    for write in writes:
        write.wait()


def pack(where, arrived, others=(), parts=1):
    count = where.shape[0]
    return pl.pallas_call(
        functools.partial(pack_kernel, parts),
        grid_spec=pltpu.PrefetchScalarGridSpec(
            num_scalar_prefetch=1,
            grid=(),
            in_specs=[pl.BlockSpec(memory_space=pltpu.HBM)] * (1 + len(others)),
            out_specs=[pl.BlockSpec(memory_space=pltpu.HBM)] * parts,
            scratch_shapes=[
                pltpu.VMEM((count, B, B), jnp.bfloat16),
                pltpu.SemaphoreType.DMA,
                pltpu.SemaphoreType.DMA((parts,)),
            ],
        ),
        out_shape=[jax.ShapeDtypeStruct((count // parts, B, B), jnp.bfloat16)] * parts,
        compiler_params=pltpu.CompilerParams(vmem_limit_bytes=ROOM),
        cost_estimate=pl.CostEstimate(
            flops=0, bytes_accessed=4 * count * B * B, transcendentals=0
        ),
        name="pack",
    )(where, arrived, *others)


def square_kernel(groups, leader, mask, left, *refs):
    out, held, done, total, sem_in, sem_out = refs[-6:]
    count = held.shape[0]

    def write(p):
        return pltpu.make_async_copy(done.at[p], out.at[p], sem_out.at[p])

    for p, inner in enumerate(refs[:count]):
        pltpu.make_async_copy(inner, held.at[p], sem_in.at[p]).start()

    @pl.loop(0, count)
    def _(p):
        pltpu.make_async_copy(refs[0], held.at[p], sem_in.at[p]).wait()
        base = groups[p] * 32
        total[...] = jnp.zeros_like(total)
        for g in range(COLS):
            for i in range(2):
                at = leader[base + i * 16 + g]
                total[i * 16 + at] += jnp.dot(
                    left[g, i],
                    held[p, g % ROWS * 4 + i * 2 + g // ROWS],
                    preferred_element_type=jnp.float32,
                )
        for n in range(32):
            kept = mask[base + n].astype(jnp.float32)
            done[p, n] = (total[n] * kept).astype(jnp.bfloat16)
        write(p).start()

    for p in range(count):
        write(p).wait()


def square(groups, leader, mask, left, inners, others):
    count = len(inners)
    hbm = pl.BlockSpec(memory_space=pltpu.HBM)
    return pl.pallas_call(
        square_kernel,
        grid_spec=pltpu.PrefetchScalarGridSpec(
            num_scalar_prefetch=3,
            grid=(),
            in_specs=[pl.BlockSpec(memory_space=pltpu.VMEM)]
            + [hbm] * (count + len(others)),
            out_specs=hbm,
            scratch_shapes=[
                pltpu.VMEM((count, 32, B, B), jnp.bfloat16),
                pltpu.VMEM((count, 32, B, B), jnp.bfloat16),
                pltpu.VMEM((32, B, B), jnp.float32),
                pltpu.SemaphoreType.DMA((count,)),
                pltpu.SemaphoreType.DMA((count,)),
            ],
        ),
        out_shape=jax.ShapeDtypeStruct((count, 32, B, B), jnp.bfloat16),
        compiler_params=pltpu.CompilerParams(vmem_limit_bytes=ROOM),
        cost_estimate=pl.CostEstimate(
            flops=count * 32 * 2 * B**3, bytes_accessed=2 * count * MIB, transcendentals=0
        ),
        name="square",
    )(groups, leader, mask, left, *inners, *others)


def cubed_kernel(is_last, groups, slots, inner_at, target, *refs):
    filtered, refs = refs[:4], refs[4:]
    count = len(refs) - 7
    pieces, (before, out, held_f, held_p, total, sem_f, sem_p) = refs[:count], refs[count:]
    steps, spare = held_f.shape[0] - 1, held_f.shape[0] - 1

    def f_start(m):
        place, core = slots[m] // 2, slots[m] % 2
        for n, blocks in enumerate(filtered):
            first = n // 2 * len(EARLY)
            found = (place >= first) & (place < first + blocks.shape[0])

            @pl.when(found & (core == n % 2))
            def _():
                pltpu.make_async_copy(
                    blocks.at[place - first], held_f.at[m], sem_f.at[m]
                ).start()

    def f_wait(m):
        pltpu.make_async_copy(filtered[0].at[0], held_f.at[m], sem_f.at[m]).wait()

    if is_last:
        last = pltpu.make_async_copy(before, total, sem_f.at[spare])
    else:
        last = pltpu.make_async_copy(filtered[0].at[0], held_f.at[spare], sem_f.at[spare])
    last.start()
    m = 0
    for piece in pieces:
        for first in range(0, piece.shape[0], GROUP):
            f_start(m)
            pltpu.make_async_copy(
                piece.at[pl.ds(first, GROUP)], held_p.at[m], sem_p.at[m]
            ).start()
            m += 1
    if is_last:
        last.wait()
    else:
        total[...] = jnp.zeros_like(total)

    @pl.loop(0, steps)
    def _(m):
        f_wait(m)
        pltpu.make_async_copy(
            pieces[0].at[pl.ds(0, GROUP)], held_p.at[m], sem_p.at[m]
        ).wait()
        base = groups[m] * 32
        for n in range(32):
            at = target[base + n] + n // 16 * GROUP
            total[at] += jnp.dot(
                held_f[m, n],
                held_p[m, inner_at[base + n]],
                preferred_element_type=jnp.float32,
            )

    if is_last:
        for i in range(2):
            for j in range(GROUP):
                out[i * B : (i + 1) * B, j * B : (j + 1) * B] = (
                    -2.0 * total[i * GROUP + j]
                ).astype(jnp.bfloat16)
    else:
        last.wait()
        own = groups[steps] * 32
        for n in range(32):
            at = inner_at[own + n] + n // 16 * GROUP
            total[at] += -1.5 * held_f[spare, n].astype(jnp.float32)
        copy = pltpu.make_async_copy(total, out, sem_f.at[spare])
        copy.start()
        copy.wait()


def cubed(groups, slots, inner_at, target, filtered, pieces, before):
    is_last = before is not None
    steps = sum(piece.shape[0] for piece in pieces) // GROUP
    if is_last:
        shape = jax.ShapeDtypeStruct((2 * B, GROUP * B), jnp.bfloat16)
        spec = pl.BlockSpec(memory_space=pltpu.VMEM)
    else:
        shape = jax.ShapeDtypeStruct((64, B, B), jnp.float32)
        spec = pl.BlockSpec(memory_space=pltpu.HBM)
        before = filtered[0]
    return pl.pallas_call(
        functools.partial(cubed_kernel, is_last),
        grid_spec=pltpu.PrefetchScalarGridSpec(
            num_scalar_prefetch=4,
            grid=(),
            in_specs=[pl.BlockSpec(memory_space=pltpu.HBM)] * (5 + len(pieces)),
            out_specs=spec,
            scratch_shapes=[
                pltpu.VMEM((steps + 1, 32, B, B), jnp.bfloat16),
                pltpu.VMEM((steps, GROUP, B, B), jnp.bfloat16),
                pltpu.VMEM((64, B, B), jnp.float32),
                pltpu.SemaphoreType.DMA((steps + 1,)),
                pltpu.SemaphoreType.DMA((steps,)),
            ],
        ),
        out_shape=shape,
        compiler_params=pltpu.CompilerParams(vmem_limit_bytes=ROOM),
        cost_estimate=pl.CostEstimate(
            flops=4 * steps * 32 * 2 * B**3,
            bytes_accessed=(2 * steps + 5) * MIB,
            transcendentals=0,
        ),
        name="cubed",
    )(groups, slots, inner_at, target, *filtered, *pieces, before)


def is_equal(values, count):
    return values[..., None] == jnp.arange(count, dtype=jnp.int32)


def picked(values, table):
    return jnp.sum(jnp.where(is_equal(values, table.shape[0]), table, 0), axis=-1)


def local(owned_blocks, owned_rows, owned_cols, keep):
    r, c = lax.axis_index("row"), lax.axis_index("col")
    tags = jnp.concatenate(
        [owned_cols.reshape(-1), owned_rows, keep.reshape(-1), jnp.zeros(688, jnp.int32)]
    )
    outgoing = spread(owned_blocks)
    arrived = lax.all_to_all(
        outgoing.reshape(ROWS * COLS, 2, B, B), AXES, split_axis=0, concat_axis=0, tiled=True
    ).reshape(256, B, B)

    tags = lax.all_to_all(
        jnp.broadcast_to(tags.reshape(1, 8, 128), (ROWS * COLS, 8, 128)),
        AXES,
        split_axis=0,
        concat_axis=0,
        tiled=True,
    )
    all_rows = tags[:, 2, :16]
    all_cols = tags[:, :2].reshape(2048, COLS)
    bands = (jnp.arange(16, dtype=jnp.int32) // 2)[None]
    ids = GROUP * (bands + ROWS * (all_rows // GROUP)) + all_rows % GROUP
    ids = jnp.where(all_rows < 64, ids, -1).reshape(2048)
    spots = (ids[None] == jnp.arange(512, dtype=jnp.int32)[:, None]).astype(jnp.bfloat16)
    cols = jnp.dot(
        spots, all_cols.astype(jnp.bfloat16), preferred_element_type=jnp.float32
    ).astype(jnp.int32)

    band_tags = lax.dynamic_slice_in_dim(all_rows, 2 * r, 2, 1).reshape(256)
    place = jnp.sum(
        jnp.where(
            band_tags[None] == jnp.arange(64, dtype=jnp.int32)[:, None],
            jnp.arange(256, dtype=jnp.int32)[None],
            0,
        ),
        axis=1,
    )
    window_cols = cols.reshape(16, GROUP, COLS)[:ROWS, :2]
    wanted = lax.dynamic_slice_in_dim(
        window_cols.reshape(ROWS, 2, 2, ROWS), r, 1, 3
    )[..., 0]
    wanted = wanted + GROUP * jnp.arange(2, dtype=jnp.int32)
    where = jnp.concatenate([picked(wanted.reshape(32), place), place[:2]])

    mine = lax.dynamic_index_in_dim(window_cols, r, 0, keepdims=False)
    rows_in = (mine + GROUP * jnp.arange(COLS, dtype=jnp.int32)[None]).reshape(32)
    tcol = (
        jnp.dot(
            is_equal(rows_in, 512).astype(jnp.bfloat16),
            cols.astype(jnp.bfloat16),
            preferred_element_type=jnp.float32,
        )
        .astype(jnp.int32)
        .reshape(2, 16, COLS)
    )
    my_cols = lax.dynamic_slice_in_dim(cols, c, 1, 1).reshape(COLS, GROUP)
    inner_at = tcol.transpose(2, 0, 1)
    target = jnp.sum(
        jnp.where(is_equal(inner_at, GROUP), my_cols[:, None, None, :], 0), axis=-1
    )
    same = inner_at[:, :, :, None] == inner_at[:, :, None, :]
    order = jnp.arange(16, dtype=jnp.int32)
    leader = jnp.min(jnp.where(same, order, 16), axis=-1)
    keep = lax.dynamic_slice_in_dim(tags[:, 2, 16:80], r * COLS, COLS, 0)
    keep = keep.reshape(COLS, 2, 1, GROUP)
    kept = jnp.sum(jnp.where(is_equal(inner_at, GROUP), keep, 0), axis=-1)
    mask = jnp.where(leader == order, kept, 0)
    leader, mask = leader.reshape(512), mask.reshape(512)

    inner, window = pack(where[:32], arrived)[0], pack(where[32:], arrived)[0]
    band = pack(place, arrived, [inner, window], 2)
    left = lax.all_gather(window, "col", axis=0, tiled=True).reshape(COLS, 2, B, B)
    inner = lax.all_to_all(
        inner.reshape(ROWS, 4, B, B), "row", split_axis=0, concat_axis=0, tiled=True
    ).reshape(32, B, B)

    p, f = {}, {(0, 0): inner}
    p[1, 0, 0] = send_row(band[0], -1, 0)
    p[3, 0, 0] = send_row(band[0], 1, 0)
    f[1, 0] = send_col(inner, -1, 0, 0)
    f[3, 0] = send_col(inner, 1, 0, 0)
    f[0, 1] = send_col(inner, 0, 1, 0)

    p[0, 0, 0], second, p[1, 0, 0], p[3, 0, 0] = after(
        [*band, p[1, 0, 0], p[3, 0, 0]], []
    )
    p[1, 0, 1] = send_row(second, -1, 0)
    p[3, 0, 1] = send_row(second, 1, 0)
    p[0, 1, 0] = send_row(p[0, 0, 0], 0, 1)
    f[1, 1] = send_col(f[0, 1], -1, 0, 0)
    f[3, 1] = send_col(f[0, 1], 1, 0, 0)

    p[0, 0, 1], p[1, 0, 0], p[3, 0, 1], p[0, 1, 0], f[1, 0], f[3, 0] = after(
        [second, p[1, 0, 0], p[3, 0, 1], p[0, 1, 0], f[1, 0], f[3, 0]],
        [p[1, 0, 1], f[0, 1], left],
    )
    p[2, 0, 0] = send_row(p[1, 0, 0], -1, 0)
    p[2, 0, 1] = send_row(p[3, 0, 1], 1, 0)
    p[0, 1, 1] = send_row(p[0, 0, 1], 0, 1)

    f[1, 0], f[3, 1] = after([f[1, 0], f[3, 1]], [f[1, 1], p[0, 0, 1]])
    f[2, 0] = send_col(f[1, 0], -1, 0, 0)
    f[2, 1] = send_col(f[3, 1], 1, 0, 0)

    keys = [(0, 1, 0), (0, 1, 1), (2, 0, 0), (2, 0, 1)]
    p.update(zip(keys, after([p[key] for key in keys], [])))
    p[1, 1, 0] = send_row(p[0, 1, 0], -1, 0)
    p[3, 1, 0] = send_row(p[0, 1, 0], 1, 0)
    p[2, 1, 0] = send_row(p[2, 0, 0], 0, 1)

    def squares(keys):
        ids = [(c // 4 + dx) % 4 * 4 + ((c % 4) ^ (2 * dz)) for dx, dz in keys]
        ids = jnp.stack(ids).astype(jnp.int32)
        return square(ids, leader, mask, left, [f[key] for key in keys], [])

    early, late, p[0, 1, 1], p[2, 0, 1] = after(
        [squares(EARLY), squares(LATE), p[0, 1, 1], p[2, 0, 1]],
        [p[1, 1, 0], p[3, 1, 0], p[2, 1, 0]],
    )
    p[1, 1, 1] = send_row(p[0, 1, 1], -1, 0)
    p[3, 1, 1] = send_row(p[0, 1, 1], 1, 0)
    p[2, 1, 1] = send_row(p[2, 0, 1], 0, 1)
    filtered = [early, send_col(early, 0, 0, 1), late, send_col(late, 0, 0, 1)]

    def products(keys, before):
        groups, slots = [], []
        for dy, dz, half in keys:
            group = (r // 2 + dy) % 4 * 2 + (r % 2 + dz) % 2 + ROWS * half
            groups.append(group)
            dx = (group // 4 - c // 4) % 4
            slots.append((dx ^ (dx // 2)) * 4 + ((group % 4) ^ (c % 4)))
        return cubed(
            jnp.stack(groups + [c]).astype(jnp.int32),
            jnp.stack(slots).astype(jnp.int32),
            inner_at.reshape(512),
            target.reshape(512),
            filtered,
            [p[key] for key in keys],
            before,
        )

    last = [(1, 1, 1), (3, 1, 1), (2, 1, 1)]
    total = products([key for key in p if key not in last], None)
    return products(last, total)


def solution(mesh):
    placed = (P(AXES, None, None, None), P(AXES), P(AXES, None), P("row", "col"))
    return jax.shard_map(
        local, mesh=mesh, in_specs=placed, out_specs=P("row", "col"), check_vma=False
    )
```

```python
import functools

import jax
import jax.numpy as jnp
from jax import lax
from jax.experimental import pallas as pl
from jax.experimental.pallas import tpu as pltpu
from jax.sharding import PartitionSpec as P

AXES = ("row", "col")
B = 128
ROWS, COLS = 8, 16
GROUP = 32
MIB = 1 << 20
ROOM = 63 * MIB
EARLY = ((0, 0), (0, 1), (1, 0), (1, 1), (3, 0), (3, 1))
LATE = ((2, 0), (2, 1))


def moved(by_y, flip_z):
    pairs = []
    for r in range(ROWS):
        y, z = r // 2, r % 2
        pairs.append((r, (y + by_y) % 4 * 2 + (z ^ flip_z)))
    return pairs


def send_col(value, by_x, flip_z, flip_core):
    pairs = []
    for n in range(COLS):
        x, z, core = n // 4, n // 2 % 2, n % 2
        pairs.append((n, (x + by_x) % 4 * 4 + (z ^ flip_z) * 2 + (core ^ flip_core)))
    return lax.ppermute(value, "col", pairs)


def send_row(value, by_y, flip_z):
    return lax.ppermute(value, "row", moved(by_y, flip_z))


def spread_kernel(owned, blocks, held, sem_in, sem_out):
    def read(n):
        return pltpu.make_async_copy(
            owned.at[n], held.at[n // 2, :, n % 2], sem_in.at[n]
        )

    def write(h):
        return pltpu.make_async_copy(held.at[h], blocks.at[h], sem_out.at[h])

    for n in range(2 * ROWS):
        read(n).start()
    for h in range(ROWS):
        read(2 * h).wait()
        read(2 * h + 1).wait()
        write(h).start()
    for h in range(ROWS):
        write(h).wait()


def spread(owned):
    return pl.pallas_call(
        spread_kernel,
        in_specs=[pl.BlockSpec(memory_space=pl.ANY)],
        out_specs=pl.BlockSpec(memory_space=pl.ANY),
        scratch_shapes=[
            pltpu.VMEM((ROWS, COLS, 2, B, B), jnp.bfloat16),
            pltpu.SemaphoreType.DMA((2 * ROWS,)),
            pltpu.SemaphoreType.DMA((ROWS,)),
        ],
        out_shape=jax.ShapeDtypeStruct((ROWS, COLS, 2, B, B), jnp.bfloat16),
        compiler_params=pltpu.CompilerParams(vmem_limit_bytes=ROOM),
        cost_estimate=pl.CostEstimate(flops=0, bytes_accessed=16 * MIB, transcendentals=0),
        name="spread",
    )(owned)


def after_kernel(*refs):
    del refs


def after(values, others):
    return pl.pallas_call(
        after_kernel,
        in_specs=[pl.BlockSpec(memory_space=pltpu.HBM)] * (len(values) + len(others)),
        out_specs=[pl.BlockSpec(memory_space=pltpu.HBM)] * len(values),
        out_shape=[jax.ShapeDtypeStruct(v.shape, v.dtype) for v in values],
        input_output_aliases={n: n for n in range(len(values))},
        compiler_params=pltpu.CompilerParams(vmem_limit_bytes=ROOM),
        cost_estimate=pl.CostEstimate(flops=0, bytes_accessed=1024, transcendentals=0),
        name="after",
    )(*values, *others)


def pack_kernel(parts, where, arrived, *refs):
    outs, held, sem, sems = refs[-3 - parts : -3], *refs[-3:]
    count = held.shape[0]

    @pl.loop(0, count)
    def _(n):
        pltpu.make_async_copy(arrived.at[where[n]], held.at[n], sem).start()

    pltpu.make_async_copy(arrived.at[pl.ds(0, count)], held, sem).wait()
    size = count // parts
    writes = [
        pltpu.make_async_copy(held.at[pl.ds(n * size, size)], out, sems.at[n])
        for n, out in enumerate(outs)
    ]
    for write in writes:
        write.start()
    for write in writes:
        write.wait()


def pack(where, arrived, others=(), parts=1):
    count = where.shape[0]
    return pl.pallas_call(
        functools.partial(pack_kernel, parts),
        grid_spec=pltpu.PrefetchScalarGridSpec(
            num_scalar_prefetch=1,
            grid=(),
            in_specs=[pl.BlockSpec(memory_space=pltpu.HBM)] * (1 + len(others)),
            out_specs=[pl.BlockSpec(memory_space=pltpu.HBM)] * parts,
            scratch_shapes=[
                pltpu.VMEM((count, B, B), jnp.bfloat16),
                pltpu.SemaphoreType.DMA,
                pltpu.SemaphoreType.DMA((parts,)),
            ],
        ),
        out_shape=[jax.ShapeDtypeStruct((count // parts, B, B), jnp.bfloat16)] * parts,
        compiler_params=pltpu.CompilerParams(vmem_limit_bytes=ROOM),
        cost_estimate=pl.CostEstimate(
            flops=0, bytes_accessed=4 * count * B * B, transcendentals=0
        ),
        name="pack",
    )(where, arrived, *others)


def square_kernel(groups, leader, mask, left, *refs):
    out, held, done, total, sem_in, sem_out = refs[-6:]
    count = held.shape[0]

    def write(p):
        return pltpu.make_async_copy(done.at[p], out.at[p], sem_out.at[p])

    for p, inner in enumerate(refs[:count]):
        pltpu.make_async_copy(inner, held.at[p], sem_in.at[p]).start()

    @pl.loop(0, count)
    def _(p):
        pltpu.make_async_copy(refs[0], held.at[p], sem_in.at[p]).wait()
        base = groups[p] * 32
        total[...] = jnp.zeros_like(total)
        for g in range(COLS):
            for i in range(2):
                at = leader[base + i * 16 + g]
                total[i * 16 + at] += jnp.dot(
                    left[g, i],
                    held[p, g % ROWS * 4 + i * 2 + g // ROWS],
                    preferred_element_type=jnp.float32,
                )
        for n in range(32):
            kept = mask[base + n].astype(jnp.float32)
            done[p, n] = (total[n] * kept).astype(jnp.bfloat16)
        write(p).start()

    for p in range(count):
        write(p).wait()


def square(groups, leader, mask, left, inners, others):
    count = len(inners)
    hbm = pl.BlockSpec(memory_space=pltpu.HBM)
    return pl.pallas_call(
        square_kernel,
        grid_spec=pltpu.PrefetchScalarGridSpec(
            num_scalar_prefetch=3,
            grid=(),
            in_specs=[pl.BlockSpec(memory_space=pltpu.VMEM)]
            + [hbm] * (count + len(others)),
            out_specs=hbm,
            scratch_shapes=[
                pltpu.VMEM((count, 32, B, B), jnp.bfloat16),
                pltpu.VMEM((count, 32, B, B), jnp.bfloat16),
                pltpu.VMEM((32, B, B), jnp.float32),
                pltpu.SemaphoreType.DMA((count,)),
                pltpu.SemaphoreType.DMA((count,)),
            ],
        ),
        out_shape=jax.ShapeDtypeStruct((count, 32, B, B), jnp.bfloat16),
        compiler_params=pltpu.CompilerParams(vmem_limit_bytes=ROOM),
        cost_estimate=pl.CostEstimate(
            flops=count * 32 * 2 * B**3, bytes_accessed=2 * count * MIB, transcendentals=0
        ),
        name="square",
    )(groups, leader, mask, left, *inners, *others)


def cubed_kernel(is_last, groups, slots, inner_at, target, *refs):
    filtered, refs = refs[:4], refs[4:]
    count = len(refs) - 7
    pieces, (before, out, held_f, held_p, total, sem_f, sem_p) = refs[:count], refs[count:]
    steps, spare = held_f.shape[0] - 1, held_f.shape[0] - 1

    def f_start(m):
        place, core = slots[m] // 2, slots[m] % 2
        for n, blocks in enumerate(filtered):
            first = n // 2 * len(EARLY)
            found = (place >= first) & (place < first + blocks.shape[0])

            @pl.when(found & (core == n % 2))
            def _():
                pltpu.make_async_copy(
                    blocks.at[place - first], held_f.at[m], sem_f.at[m]
                ).start()

    def f_wait(m):
        pltpu.make_async_copy(filtered[0].at[0], held_f.at[m], sem_f.at[m]).wait()

    if is_last:
        last = pltpu.make_async_copy(before, total, sem_f.at[spare])
    else:
        last = pltpu.make_async_copy(filtered[0].at[0], held_f.at[spare], sem_f.at[spare])
    last.start()
    m = 0
    for piece in pieces:
        for first in range(0, piece.shape[0], GROUP):
            f_start(m)
            pltpu.make_async_copy(
                piece.at[pl.ds(first, GROUP)], held_p.at[m], sem_p.at[m]
            ).start()
            m += 1
    if is_last:
        last.wait()
    else:
        total[...] = jnp.zeros_like(total)

    @pl.loop(0, steps)
    def _(m):
        f_wait(m)
        pltpu.make_async_copy(
            pieces[0].at[pl.ds(0, GROUP)], held_p.at[m], sem_p.at[m]
        ).wait()
        base = groups[m] * 32
        for n in range(32):
            at = target[base + n] + n // 16 * GROUP
            total[at] += jnp.dot(
                held_f[m, n],
                held_p[m, inner_at[base + n]],
                preferred_element_type=jnp.float32,
            )

    if is_last:
        for i in range(2):
            for j in range(GROUP):
                out[i * B : (i + 1) * B, j * B : (j + 1) * B] = (
                    -2.0 * total[i * GROUP + j]
                ).astype(jnp.bfloat16)
    else:
        last.wait()
        own = groups[steps] * 32
        for n in range(32):
            at = inner_at[own + n] + n // 16 * GROUP
            total[at] += -1.5 * held_f[spare, n].astype(jnp.float32)
        copy = pltpu.make_async_copy(total, out, sem_f.at[spare])
        copy.start()
        copy.wait()


def cubed(groups, slots, inner_at, target, filtered, pieces, before):
    is_last = before is not None
    steps = sum(piece.shape[0] for piece in pieces) // GROUP
    if is_last:
        shape = jax.ShapeDtypeStruct((2 * B, GROUP * B), jnp.bfloat16)
        spec = pl.BlockSpec(memory_space=pltpu.VMEM)
    else:
        shape = jax.ShapeDtypeStruct((64, B, B), jnp.float32)
        spec = pl.BlockSpec(memory_space=pltpu.HBM)
        before = filtered[0]
    return pl.pallas_call(
        functools.partial(cubed_kernel, is_last),
        grid_spec=pltpu.PrefetchScalarGridSpec(
            num_scalar_prefetch=4,
            grid=(),
            in_specs=[pl.BlockSpec(memory_space=pltpu.HBM)] * (5 + len(pieces)),
            out_specs=spec,
            scratch_shapes=[
                pltpu.VMEM((steps + 1, 32, B, B), jnp.bfloat16),
                pltpu.VMEM((steps, GROUP, B, B), jnp.bfloat16),
                pltpu.VMEM((64, B, B), jnp.float32),
                pltpu.SemaphoreType.DMA((steps + 1,)),
                pltpu.SemaphoreType.DMA((steps,)),
            ],
        ),
        out_shape=shape,
        compiler_params=pltpu.CompilerParams(vmem_limit_bytes=ROOM),
        cost_estimate=pl.CostEstimate(
            flops=4 * steps * 32 * 2 * B**3,
            bytes_accessed=(2 * steps + 5) * MIB,
            transcendentals=0,
        ),
        name="cubed",
    )(groups, slots, inner_at, target, *filtered, *pieces, before)


def is_equal(values, count):
    return values[..., None] == jnp.arange(count, dtype=jnp.int32)


def picked(values, table):
    return jnp.sum(jnp.where(is_equal(values, table.shape[0]), table, 0), axis=-1)


def local(owned_blocks, owned_rows, owned_cols, keep):
    r, c = lax.axis_index("row"), lax.axis_index("col")
    tags = jnp.concatenate(
        [owned_cols.reshape(-1), owned_rows, keep.reshape(-1), jnp.zeros(688, jnp.int32)]
    )
    outgoing = spread(owned_blocks)
    arrived = lax.all_to_all(
        outgoing.reshape(ROWS * COLS, 2, B, B), AXES, split_axis=0, concat_axis=0, tiled=True
    ).reshape(256, B, B)

    tags = lax.all_to_all(
        jnp.broadcast_to(tags.reshape(1, 8, 128), (ROWS * COLS, 8, 128)),
        AXES,
        split_axis=0,
        concat_axis=0,
        tiled=True,
    )
    all_rows = tags[:, 2, :16]
    all_cols = tags[:, :2].reshape(2048, COLS)
    bands = (jnp.arange(16, dtype=jnp.int32) // 2)[None]
    ids = GROUP * (bands + ROWS * (all_rows // GROUP)) + all_rows % GROUP
    ids = jnp.where(all_rows < 64, ids, -1).reshape(2048)
    spots = (ids[None] == jnp.arange(512, dtype=jnp.int32)[:, None]).astype(jnp.bfloat16)
    cols = jnp.dot(
        spots, all_cols.astype(jnp.bfloat16), preferred_element_type=jnp.float32
    ).astype(jnp.int32)

    band_tags = lax.dynamic_slice_in_dim(all_rows, 2 * r, 2, 1).reshape(256)
    place = jnp.sum(
        jnp.where(
            band_tags[None] == jnp.arange(64, dtype=jnp.int32)[:, None],
            jnp.arange(256, dtype=jnp.int32)[None],
            0,
        ),
        axis=1,
    )
    window_cols = cols.reshape(16, GROUP, COLS)[:ROWS, :2]
    wanted = lax.dynamic_slice_in_dim(
        window_cols.reshape(ROWS, 2, 2, ROWS), r, 1, 3
    )[..., 0]
    wanted = wanted + GROUP * jnp.arange(2, dtype=jnp.int32)
    where = jnp.concatenate([picked(wanted.reshape(32), place), place[:2]])

    mine = lax.dynamic_index_in_dim(window_cols, r, 0, keepdims=False)
    rows_in = (mine + GROUP * jnp.arange(COLS, dtype=jnp.int32)[None]).reshape(32)
    tcol = (
        jnp.dot(
            is_equal(rows_in, 512).astype(jnp.bfloat16),
            cols.astype(jnp.bfloat16),
            preferred_element_type=jnp.float32,
        )
        .astype(jnp.int32)
        .reshape(2, 16, COLS)
    )
    my_cols = lax.dynamic_slice_in_dim(cols, c, 1, 1).reshape(COLS, GROUP)
    inner_at = tcol.transpose(2, 0, 1)
    target = jnp.sum(
        jnp.where(is_equal(inner_at, GROUP), my_cols[:, None, None, :], 0), axis=-1
    )
    same = inner_at[:, :, :, None] == inner_at[:, :, None, :]
    order = jnp.arange(16, dtype=jnp.int32)
    leader = jnp.min(jnp.where(same, order, 16), axis=-1)
    keep = lax.dynamic_slice_in_dim(tags[:, 2, 16:80], r * COLS, COLS, 0)
    keep = keep.reshape(COLS, 2, 1, GROUP)
    kept = jnp.sum(jnp.where(is_equal(inner_at, GROUP), keep, 0), axis=-1)
    mask = jnp.where(leader == order, kept, 0)
    leader, mask = leader.reshape(512), mask.reshape(512)

    inner, window = pack(where[:32], arrived)[0], pack(where[32:], arrived)[0]
    band = pack(place, arrived, [inner], 2)
    left = lax.all_gather(window, "col", axis=0, tiled=True).reshape(COLS, 2, B, B)
    inner = lax.all_to_all(
        inner.reshape(ROWS, 4, B, B), "row", split_axis=0, concat_axis=0, tiled=True
    ).reshape(32, B, B)

    p, f = {}, {(0, 0): inner}
    p[1, 0, 0] = send_row(band[0], -1, 0)
    p[3, 0, 0] = send_row(band[0], 1, 0)
    f[1, 0] = send_col(inner, -1, 0, 0)
    f[3, 0] = send_col(inner, 1, 0, 0)
    f[0, 1] = send_col(inner, 0, 1, 0)

    p[0, 0, 0], second, p[1, 0, 0], p[3, 0, 0] = after(
        [*band, p[1, 0, 0], p[3, 0, 0]], []
    )
    p[1, 0, 1] = send_row(second, -1, 0)
    p[3, 0, 1] = send_row(second, 1, 0)
    p[0, 1, 0] = send_row(p[0, 0, 0], 0, 1)
    f[1, 1] = send_col(f[0, 1], -1, 0, 0)
    f[3, 1] = send_col(f[0, 1], 1, 0, 0)

    p[0, 0, 1], p[1, 0, 0], p[3, 0, 1], p[0, 1, 0], f[1, 0], f[3, 0] = after(
        [second, p[1, 0, 0], p[3, 0, 1], p[0, 1, 0], f[1, 0], f[3, 0]],
        [p[1, 0, 1], f[0, 1], left],
    )
    p[2, 0, 0] = send_row(p[1, 0, 0], -1, 0)
    p[2, 0, 1] = send_row(p[3, 0, 1], 1, 0)
    p[0, 1, 1] = send_row(p[0, 0, 1], 0, 1)

    f[1, 0], f[3, 1] = after([f[1, 0], f[3, 1]], [f[1, 1], p[0, 0, 1]])
    f[2, 0] = send_col(f[1, 0], -1, 0, 0)
    f[2, 1] = send_col(f[3, 1], 1, 0, 0)

    keys = [(0, 1, 0), (0, 1, 1), (2, 0, 0), (2, 0, 1)]
    p.update(zip(keys, after([p[key] for key in keys], [])))
    p[1, 1, 0] = send_row(p[0, 1, 0], -1, 0)
    p[3, 1, 0] = send_row(p[0, 1, 0], 1, 0)
    p[2, 1, 0] = send_row(p[2, 0, 0], 0, 1)

    def squares(keys):
        ids = [(c // 4 + dx) % 4 * 4 + ((c % 4) ^ (2 * dz)) for dx, dz in keys]
        ids = jnp.stack(ids).astype(jnp.int32)
        return square(ids, leader, mask, left, [f[key] for key in keys], [])

    early, late, p[0, 1, 1], p[2, 0, 1] = after(
        [squares(EARLY), squares(LATE), p[0, 1, 1], p[2, 0, 1]],
        [p[1, 1, 0], p[3, 1, 0], p[2, 1, 0]],
    )
    p[1, 1, 1] = send_row(p[0, 1, 1], -1, 0)
    p[3, 1, 1] = send_row(p[0, 1, 1], 1, 0)
    p[2, 1, 1] = send_row(p[2, 0, 1], 0, 1)
    filtered = [early, send_col(early, 0, 0, 1), late, send_col(late, 0, 0, 1)]

    def products(keys, before):
        groups, slots = [], []
        for dy, dz, half in keys:
            group = (r // 2 + dy) % 4 * 2 + (r % 2 + dz) % 2 + ROWS * half
            groups.append(group)
            dx = (group // 4 - c // 4) % 4
            slots.append((dx ^ (dx // 2)) * 4 + ((group % 4) ^ (c % 4)))
        return cubed(
            jnp.stack(groups + [c]).astype(jnp.int32),
            jnp.stack(slots).astype(jnp.int32),
            inner_at.reshape(512),
            target.reshape(512),
            filtered,
            [p[key] for key in keys],
            before,
        )

    last = [(1, 1, 1), (3, 1, 1), (2, 1, 1)]
    total = products([key for key in p if key not in last], None)
    return products(last, total)


def solution(mesh):
    placed = (P(AXES, None, None, None), P(AXES), P(AXES, None), P("row", "col"))
    return jax.shard_map(
        local, mesh=mesh, in_specs=placed, out_specs=P("row", "col"), check_vma=False
    )
```
